512 devices in a mesh: replica: 32 (over z, x_lo), fsdp: 16 (over x_hi, y, core).
Axes of the slice: x: 4 (x_hi: 2, x_lo: 2; x = x_hi * 2 + x_lo), y: 4, z: 16, core: 2. Of those that a mesh axis runs over, the one named last changes fastest.
Arguments:
- tokens: bfloat16 [32, 2048, 8192], P('replica', 'fsdp'), may hold values from -6 to 6
- norm_gain: float32 [8192], replicated, may hold values from 0.1 to 1.9
- weight: bfloat16 [32, 8192, 768], P('replica', 'fsdp'), may hold values from -0.0625 to 0.0625
- momentum: float32 [32, 8192, 128], P('replica', 'fsdp'), may hold values from -0.03 to 0.03
- cotangent: bfloat16 [32, 2048, 768], P('replica', 'fsdp'), may hold values from -6 to 6
- fragment: int32 [32], replicated, may hold values from 0 to 5
- partner: int32 [32], replicated, may hold values from 0 to 31, as said below
Outputs:
- keys: bfloat16 [32, 2048, 768], P('replica', 'fsdp')
- new_weight: bfloat16 [32, 8192, 768], P('replica', 'fsdp')
- new_momentum: float32 [32, 8192, 128], P('replica', 'fsdp')
The draws below stay inside these ranges and needn't reach their ends.
Inputs may be any that keep to these rules, and one draw needn't show every extreme that they name: partner is a perfect matching: partner[partner[r]] == r and partner[r] != r.
All inputs are finite; a program needn't handle non-finite values.
Results may differ from the reference program's by a relative error of at most 0.0049.
Values may be sent and summed in bfloat16 or wider, within the bound.
A program may use at most 128 MiB of HBM per device.

```python
import jax
import jax.numpy as jnp
from jax import lax

D = 8192
HD = 128
KVW = 768
TOK_REP = 2048
FRAGS = 6
REPLICAS = 32


def draw_partner(key, part):
    key = jax.random.fold_in(key, 11)
    shuffled = jax.random.permutation(key, REPLICAS).astype(jnp.int32)
    mates = shuffled[jnp.arange(REPLICAS, dtype=jnp.int32) ^ 1]
    return jnp.zeros((REPLICAS,), jnp.int32).at[shuffled].set(mates)


def with_ends(drawn, stream_key, least, top_value):
    index_at = [jax.random.randint(jax.random.fold_in(stream_key, axis), (), 0, length) for axis, length in enumerate(drawn.shape)]
    main_axis = drawn.shape.index(max(drawn.shape))
    beside = index_at[:main_axis] + [(index_at[main_axis] + 1) % drawn.shape[main_axis]] + index_at[main_axis + 1:]
    return drawn.at[tuple(index_at)].set(least).at[tuple(beside)].set(top_value)


def steps_of(rng, shape, shards, smallest, high):
    def one(axis_at, blocks):
        draws = jax.random.uniform(jax.random.fold_in(jax.random.fold_in(rng, 6), axis_at), (blocks,), jnp.float32, smallest / len(shards), high / len(shards))
        return jnp.repeat(jnp.exp(draws), shape[axis_at] // blocks).reshape((-1,) + (1,) * (len(shape) - axis_at - 1))

    level = one(*shards[0])
    for cut in shards[1:]:
        level = level * one(*cut)
    return level


def gaussian(own_key, dims, spread, bound, split=(), held_as=jnp.bfloat16):
    values = spread * jax.random.normal(own_key, dims, jnp.float32)
    if split:
        values = values * steps_of(own_key, dims, split, -0.22, 0.18)
    return jnp.clip(values, -bound, bound).astype(held_as)


def setup_inputs(seed: int = 0) -> dict:
    seeds = jax.random.split(jax.random.key(seed), 8)
    return {
        "tokens": gaussian(seeds[0], (REPLICAS, TOK_REP, D), 1.0, 6.0, ((0, 32), (1, 16))),
        "norm_gain": jnp.clip(1.0 + 0.18 * jax.random.normal(seeds[1], (D,), jnp.float32), 0.1, 1.9),
        "weight": gaussian(seeds[2], (REPLICAS, D, KVW), D ** -0.5, 0.0625, ((0, 32), (1, 16))),
        "momentum": gaussian(seeds[3], (REPLICAS, D, HD), 0.005, 0.03, ((0, 32), (1, 16)), jnp.float32),
        "cotangent": gaussian(seeds[4], (REPLICAS, TOK_REP, KVW), 1.0, 6.0, ((0, 32), (1, 16))),
        "fragment": with_ends(jax.random.randint(seeds[5], (REPLICAS,), 0, FRAGS), jax.random.fold_in(seeds[5], 1), 0, FRAGS - 1).astype(jnp.int32),
        "partner": draw_partner(jax.random.fold_in(seeds[7], 71), 0),
    }


inner_rate = 0.0001
outer_rate = 0.7
beta_value = 0.9

def reference(tokens, norm_gain, weight, momentum, cotangent, fragment, partner):

    def one_replica(items):
        rows, matrix, grads_in = items
        values = rows.astype(jnp.float32)
        scale = lax.rsqrt(lax.optimization_barrier(jnp.mean(values * values, axis=-1, keepdims=True)) + 1e-05)
        normed = (values * scale * norm_gain).astype(jnp.bfloat16)
        keys = jnp.dot(normed, matrix, preferred_element_type=jnp.float32).astype(jnp.bfloat16)
        grad = jnp.dot(normed.T, grads_in, preferred_element_type=jnp.float32)
        return (keys, grad)
    keys, grads = lax.map(one_replica, (tokens, weight, cotangent))
    owners = jnp.arange(REPLICAS, dtype=jnp.int32)
    lower = jnp.minimum(owners, partner.astype(jnp.int32))
    offsets = (fragment[lower] * HD).astype(jnp.int32)

    def cut(matrix, offset):
        return lax.dynamic_slice_in_dim(matrix, offset, HD, 1)

    def paste(matrix, piece, offset):
        return lax.dynamic_update_slice_in_dim(matrix, piece, offset, 1)
    frag_grad = jax.vmap(cut)(grads, offsets)
    delta = (inner_rate * frag_grad).astype(jnp.bfloat16)
    mix = (delta.astype(jnp.float32) + delta[partner].astype(jnp.float32)) * 0.5
    new_momentum = beta_value * momentum + mix
    anchor = weight.astype(jnp.float32)
    inner = anchor - inner_rate * grads
    frag_anchor = jax.vmap(cut)(anchor, offsets)
    outer = frag_anchor - outer_rate * (beta_value * new_momentum + mix)
    new_weight = jax.vmap(paste)(inner, outer, offsets).astype(jnp.bfloat16)
    return (keys, new_weight, new_momentum)
```

```python
import jax
import jax.numpy as jnp
from jax import lax
from jax.experimental import pallas as pl
from jax.experimental.pallas import tpu as pltpu
from jax.sharding import PartitionSpec as P

HD = 128
NC = 4
MESH = pl.DeviceIdType.MESH
F32 = jnp.float32
BF16 = jnp.bfloat16

inner_rate = 0.0001
outer_rate = 0.7
beta_value = 0.9


def kernel(
    tokens, gain, weight, momentum, cot, fragment, partner_row, partner,
    keys_o, nw_o, nm_o,
    tok, scale, S, R, W2, C, Gt, Gs, Gr, Pacc, Ps, Pr, Ss, Sr, D, X1, X2s, X2r, mom, fragv,
    lsem, a_s, a_r, w_s, w_r, c_s, c_r, f_s, f_r, g_s, g_r, p_s, p_r, k_s, k_r, x1_s, x1_r, x2_s, x2_r,
):
    r = lax.axis_index("replica")
    f = lax.axis_index("fsdp")
    xh = f // 8
    q = f % 8
    y = q // 2
    c = q % 2
    z = r // 2

    def dev(q2):
        return (r, xh * 8 + q2)

    xpart = (r, (1 - xh) * 8 + q)
    sib = dev(y * 2 + 1 - c)

    tok_cp = [
        pltpu.make_async_copy(tokens.at[pl.ds(h * 32, 32)], tok.at[pl.ds(h * 32, 32)], lsem.at[h])
        for h in range(4)
    ]
    c_cp = pltpu.make_async_copy(cot, C.at[q], lsem.at[4])
    w_cp = pltpu.make_async_copy(weight, W2.at[:, xh], lsem.at[5])
    m_cp = pltpu.make_async_copy(momentum, mom, lsem.at[6])
    c_cp.start()
    w_cp.start()
    for cp in tok_cp:
        cp.start()
    m_cp.start()

    bar = pltpu.get_barrier_semaphore()
    for k in range(1, 8):
        pl.semaphore_signal(bar, inc=1, device_id=dev((q + k) % 8), device_id_type=MESH)
    pl.semaphore_signal(bar, inc=1, device_id=xpart, device_id_type=MESH)

    def greet(k, _):
        pl.semaphore_signal(bar, inc=1, device_id=((r + k) % 32, f), device_id_type=MESH)
        return 0

    lax.fori_loop(1, 32, greet, 0)
    pl.semaphore_wait(bar, 39)

    def c_send(k):
        if k == 0:
            to = sib
        else:
            to = dev(((y + k) % 4) * 2 + c)
        return pltpu.make_async_remote_copy(
            src_ref=C.at[q], dst_ref=C.at[q], send_sem=c_s.at[k], recv_sem=c_r.at[k], device_id=to, device_id_type=MESH)

    c_cp.wait()
    for k in (2, 1, 3, 0):
        c_send(k).start()

    def w_send(i):
        return pltpu.make_async_remote_copy(
            src_ref=W2.at[i, xh], dst_ref=W2.at[i, xh], send_sem=w_s.at[i], recv_sem=w_r.at[i], device_id=xpart,
            device_id_type=MESH)

    w_cp.wait()
    for i in range(NC):
        w_send(i).start()

    for cp in tok_cp:
        cp.wait()

    def rows(t, _):
        v = tok[pl.ds(pl.multiple_of(t * 16, 16), 16), :].astype(F32)
        m = jnp.sum(v * v, axis=-1, keepdims=True) * (1.0 / 8192)
        scale[pl.ds(pl.multiple_of(t * 16, 16), 16), :] = jnp.broadcast_to(lax.rsqrt(m + 1e-05), (16, 128))
        return 0

    lax.fori_loop(0, 8, rows, 0)

    def a_send(i, k):
        q2 = (q + k) % 8
        return pltpu.make_async_remote_copy(
            src_ref=S.at[i, q2], dst_ref=R.at[i, q], send_sem=a_s.at[i, k], recv_sem=a_r.at[i, k], device_id=dev(q2),
            device_id_type=MESH)

    def norm_chunk(i):
        def one(b, _):
            for h in range(2):
                col = pl.multiple_of(h * 4096 + b * 512 + i * 128, 128)
                v = tok[:, pl.ds(col, 128)].astype(F32)
                S[i, b, :, h * 128:(h + 1) * 128] = (v * scale[...] * gain[:, pl.ds(col, 128)]).astype(BF16)
            return 0

        lax.fori_loop(0, 8, one, 0)
        R[i, q] = S[i, q]

    def send_chunk(i):
        def one(k, _):
            a_send(i, k).start()
            return 0

        lax.fori_loop(1, 8, one, 0)

    for i in range(NC):
        norm_chunk(i)
        if i < 2:
            send_chunk(i)

    def c_pass(k):
        slot = ((y + 4 - k) % 4) * 2 + c
        return pltpu.make_async_remote_copy(
            src_ref=C.at[slot], dst_ref=C.at[slot], send_sem=f_s.at[k], recv_sem=f_r.at[k], device_id=sib,
            device_id_type=MESH)

    for k in (1, 3, 2):
        c_send(k).wait_recv()
        c_pass(k).start()
    c_send(0).wait_recv()
    for k in (1, 3, 2):
        c_pass(k).wait_recv()

    lane = lax.broadcasted_iota(jnp.int32, (8, 32), 1).astype(F32)
    mine = r.astype(F32)
    partners = jnp.broadcast_to(partner_row[...].astype(F32), (8, 32))
    mate = jnp.sum(jnp.where(lane == mine, partners, 0.0), axis=-1, keepdims=True)
    fragments = jnp.broadcast_to(fragment[...].astype(F32), (8, 32))
    frag_at = jnp.sum(jnp.where(lane == jnp.minimum(mate, mine), fragments, 0.0), axis=-1, keepdims=True)
    fragv[...] = jnp.broadcast_to(frag_at, (8, HD))

    def g_send(i):
        return pltpu.make_async_remote_copy(
            src_ref=Gs.at[i], dst_ref=Gr.at[i], send_sem=g_s.at[i], recv_sem=g_r.at[i], device_id=xpart,
            device_id_type=MESH)

    def x1_send(i, k):
        j = 8 * (k // 2) + 2 * i + k % 2
        return j, pltpu.make_async_remote_copy(
            src_ref=D.at[i, k], dst_ref=X1.at[r], send_sem=x1_s, recv_sem=x1_r, device_id=(j, f), device_id_type=MESH)

    def finalize(i):
        g_send(i).wait_recv()
        Gt[i, xh] = Gt[i, xh] + Gr[i].astype(F32)
        frag = jnp.broadcast_to(fragv[0:1, :], (128, HD))
        cut = Gt[i, xh, :, 0:HD]
        for j in range(1, 6):
            cut = jnp.where(frag == float(j), Gt[i, xh, :, j * HD:(j + 1) * HD], cut)
        d = (inner_rate * cut).astype(BF16)
        D[i] = d.reshape(8, 16, HD)

        def one(k, _):
            j, cp = x1_send(i, k)

            @pl.when(j != r)
            def _():
                cp.start()

            @pl.when(j == r)
            def _():
                X1[r] = D[i, k]

            return 0

        lax.fori_loop(0, 8, one, 0)

    my_piece = 2 * (z // 4) + r % 2
    my_chunk = z % 4

    def x2_send(k):
        d = (r + k) % 32
        return pltpu.make_async_remote_copy(
            src_ref=X2s.at[d], dst_ref=X2r.at[my_chunk, my_piece], send_sem=x2_s, recv_sem=x2_r.at[my_chunk],
            device_id=(d, f), device_id_type=MESH)

    def relay(i):
        @pl.when(my_chunk == i)
        def _():
            whole = X1.at[pl.ds(0, 31)]
            pltpu.make_async_copy(whole, whole, x1_r).wait()

            def pick(d, _):
                X2s[d] = X1[partner[d]]
                return 0

            lax.fori_loop(0, 32, pick, 0)

            def one(k, _):
                x2_send(k).start()
                return 0

            lax.fori_loop(1, 32, one, 0)
            X2r[i, my_piece] = X2s[r]

    def step(t, _):
        def arrive(k, _):
            a_send(t, k).wait_recv()
            return 0

        lax.fori_loop(1, 8, arrive, 0)

        @pl.when(t < NC - 2)
        def _():
            send_chunk(t + 2)

        lhs = R[t].reshape(1024, 256)
        for n in range(3):
            cols = slice(n * 256, (n + 1) * 256)
            g = lax.dot_general(lhs, C[:, :, cols].reshape(1024, 256), (((0,), (0,)), ((), ())), preferred_element_type=F32)
            Gt[t, :, :, cols] = g.reshape(2, 128, 256)
        Gs[t] = Gt[t, 1 - xh].astype(BF16)
        g_send(t).start()

        @pl.when(t >= 1)
        def _():
            finalize(t - 1)

        @pl.when(t >= 2)
        def _():
            relay(t - 2)

        w_send(t).wait_recv()

        @pl.when(t == 0)
        def _():
            Pacc[...] = jnp.zeros_like(Pacc)

        for n in range(3):
            cols = slice(n * 256, (n + 1) * 256)
            p = jnp.dot(lhs, W2[t, :, :, cols].reshape(256, 256), preferred_element_type=F32)
            Pacc[:, :, cols] += p.reshape(8, 128, 256)
        return 0

    lax.fori_loop(0, NC, step, 0)

    p_send = pltpu.make_async_remote_copy(
        src_ref=Ps, dst_ref=Pr, send_sem=p_s, recv_sem=p_r, device_id=sib, device_id_type=MESH)
    for b in range(4):
        Ps[b] = Pacc[b * 2 + 1 - c].astype(BF16)
    p_send.start()
    finalize(NC - 1)
    relay(NC - 2)

    def k_send(k):
        y2 = (y + k) % 4
        return pltpu.make_async_remote_copy(
            src_ref=Ss.at[y2], dst_ref=Sr.at[k - 1], send_sem=k_s.at[k], recv_sem=k_r.at[k], device_id=dev(y2 * 2 + c),
            device_id_type=MESH)

    p_send.wait_recv()
    for k in (2, 1, 3):
        y2 = (y + k) % 4
        Ss[y2] = (Pacc[y2 * 2 + c] + Pr[y2].astype(F32)).astype(BF16)
        k_send(k).start()
    own = Pacc[q] + Pr[y].astype(F32)
    relay(NC - 1)

    m_cp.wait()
    for k in (1, 3, 2):
        k_send(k).wait_recv()
    keys_o[...] = (own + Sr[0].astype(F32) + Sr[1].astype(F32) + Sr[2].astype(F32)).astype(BF16)

    def update(i, _):
        @pl.when(my_chunk == i)
        def _():
            part = X2r.at[i, pl.ds(0, 7)]
            pltpu.make_async_copy(part, part, x2_r.at[i]).wait()

        @pl.when(my_chunk != i)
        def _():
            part = X2r.at[i]
            pltpu.make_async_copy(part, part, x2_r.at[i]).wait()

        here = pl.ds(pl.multiple_of(i * 128, 128), 128)
        delta = D[i].reshape(128, HD).astype(F32)
        mix = (delta + X2r[i].reshape(128, HD).astype(F32)) * 0.5
        nm = beta_value * mom[here, :] + mix
        nm_o[here, :] = nm
        frag = jnp.broadcast_to(fragv[0:1, :], (128, HD))
        step_out = outer_rate * (beta_value * nm + mix)
        for j in range(6):
            cols = slice(j * HD, (j + 1) * HD)
            change = jnp.where(frag == float(j), step_out, inner_rate * Gt[i, xh, :, cols])
            nw_o[here, cols] = (W2[i, xh, :, cols].astype(F32) - change).astype(BF16)
        return 0

    lax.fori_loop(0, NC, update, 0)

    for k in range(4):
        c_send(k).wait_send()
    for k in (1, 2, 3):
        c_pass(k).wait_send()
        k_send(k).wait_send()
    p_send.wait_send()

    def sent(i, _):
        w_send(i).wait_send()
        g_send(i).wait_send()

        def one(k, _):
            a_send(i, k).wait_send()
            return 0

        lax.fori_loop(1, 8, one, 0)
        return 0

    lax.fori_loop(0, NC, sent, 0)
    most = X1.at[pl.ds(0, 31)]
    pltpu.make_async_copy(most, most, x1_s).wait()
    pltpu.make_async_copy(most, most, x2_s).wait()


def body(tokens, norm_gain, weight, momentum, cotangent, fragment, partner):
    any_, vmem, smem = (pl.BlockSpec(memory_space=m) for m in (pl.ANY, pltpu.VMEM, pltpu.SMEM))
    V = pltpu.VMEM
    dma = pltpu.SemaphoreType.DMA
    keys, nw, nm = pl.pallas_call(
        kernel,
        out_shape=(
            jax.ShapeDtypeStruct((128, 768), BF16),
            jax.ShapeDtypeStruct((512, 768), BF16),
            jax.ShapeDtypeStruct((512, HD), F32),
        ),
        in_specs=[any_, vmem, any_, any_, any_, vmem, vmem, smem],
        out_specs=(vmem, vmem, vmem),
        scratch_shapes=[
            V((128, 8192), BF16),
            V((128, 128), F32),
            V((NC, 8, 128, 256), BF16),
            V((NC, 8, 128, 256), BF16),
            V((NC, 2, 128, 768), BF16),
            V((8, 128, 768), BF16),
            V((NC, 2, 128, 768), F32),
            V((NC, 128, 768), BF16),
            V((NC, 128, 768), BF16),
            V((8, 128, 768), F32),
            V((4, 128, 768), BF16),
            V((4, 128, 768), BF16),
            V((4, 128, 768), BF16),
            V((3, 128, 768), BF16),
            V((NC, 8, 16, HD), BF16),
            V((32, 16, HD), BF16),
            V((32, 16, HD), BF16),
            V((NC, 8, 16, HD), BF16),
            V((512, HD), F32),
            V((8, HD), F32),
            dma((7,)),
            dma((NC, 8)), dma((NC, 8)),
            dma((NC,)), dma((NC,)),
            dma((4,)), dma((4,)),
            dma((4,)), dma((4,)),
            dma((NC,)), dma((NC,)),
            dma, dma,
            dma((4,)), dma((4,)),
            dma, dma,
            dma, dma((NC,)),
        ],
        compiler_params=pltpu.CompilerParams(
            collective_id=0, has_side_effects=True, vmem_limit_bytes=48 * 2**20
        ),
    )(tokens[0], norm_gain[None], weight[0].reshape(NC, 128, 768), momentum[0], cotangent[0], fragment[None], partner[None], partner)
    return (keys[None], nw[None], nm[None])


def solution(mesh):
    in_specs = (
        P("replica", "fsdp", None),
        P(),
        P("replica", "fsdp", None),
        P("replica", "fsdp", None),
        P("replica", "fsdp", None),
        P(),
        P(),
    )
    out_specs = (P("replica", "fsdp", None), P("replica", "fsdp", None), P("replica", "fsdp", None))
    return jax.shard_map(body, mesh=mesh, in_specs=in_specs, out_specs=out_specs, check_vma=False)
```

```python
import jax
import jax.numpy as jnp
from jax import lax
from jax.experimental import pallas as pl
from jax.experimental.pallas import tpu as pltpu
from jax.sharding import PartitionSpec as P

HD = 128
NC = 4
NA = 2
MESH = pl.DeviceIdType.MESH
F32 = jnp.float32
BF16 = jnp.bfloat16

inner_rate = 0.0001
outer_rate = 0.7
beta_value = 0.9


def kernel(
    tokens, gain_h, weight, momentum, cot, fragment_h, partner_h,
    keys_o, nw_o, nm_o,
    tok, scale, S, R, W2, Cl, Cf, Ca, Cb, Gtf, Gta, Gtb, Gsf, Gsa, Gsb, Grf, Gra, Grb, Pacc, Ps, Pr, Ss, Sr,
    D, X1, X2s, X2r, mom, fragv, gain, fragment, partner_row, partner, keys_v, nw_v, nm_v,
    lsem, a_s, a_r, w_s, w_r, c_s, c_r, f_s, f_r, g_s, g_r, p_s, p_r, k_s, k_r, x1_s, x1_r, x2_s, x2_r,
):
    r = lax.axis_index("replica")
    f = lax.axis_index("fsdp")
    xh = f // 8
    q = f % 8
    y = q // 2
    c = q % 2
    z = r // 2
    C = (Cf, Ca, Cb)
    Gt = (Gtf, Gta, Gtb)
    Gs = (Gsf, Gsa, Gsb)
    Gr = (Grf, Gra, Grb)

    def dev(q2):
        return (r, xh * 8 + q2)

    xpart = (r, (1 - xh) * 8 + q)
    sib = dev(y * 2 + 1 - c)

    small = [
        pltpu.make_async_copy(a, b, lsem.at[n])
        for n, (a, b) in enumerate(((fragment_h, fragment), (partner_h, partner_row), (partner_h, partner), (gain_h, gain)))
    ]
    c_cp = pltpu.make_async_copy(cot, Cl, lsem.at[4])
    w_cp = pltpu.make_async_copy(weight, W2.at[:, xh], lsem.at[5])
    m_cp = pltpu.make_async_copy(momentum, mom, lsem.at[6])
    tok_cp = [
        pltpu.make_async_copy(tokens.at[pl.ds(h * 32, 32)], tok.at[pl.ds(h * 32, 32)], lsem.at[7 + h])
        for h in range(4)
    ]
    for cp in [*small, c_cp, *tok_cp, w_cp, m_cp]:
        cp.start()

    bar = pltpu.get_barrier_semaphore()
    for k in range(1, 8):
        pl.semaphore_signal(bar, inc=1, device_id=dev((q + k) % 8), device_id_type=MESH)
    pl.semaphore_signal(bar, inc=1, device_id=xpart, device_id_type=MESH)

    def greet(k, _):
        pl.semaphore_signal(bar, inc=1, device_id=((r + k) % 32, f), device_id_type=MESH)
        return 0

    lax.fori_loop(1, 32, greet, 0)

    for cp in small:
        cp.wait()
    lane = lax.broadcasted_iota(jnp.int32, (8, 32), 1).astype(F32)
    mine = r.astype(F32)
    partners = jnp.broadcast_to(partner_row[...].astype(F32), (8, 32))
    mate = jnp.sum(jnp.where(lane == mine, partners, 0.0), axis=-1, keepdims=True)
    fragments = jnp.broadcast_to(fragment[...].astype(F32), (8, 32))
    frag_at = jnp.sum(jnp.where(lane == jnp.minimum(mate, mine), fragments, 0.0), axis=-1, keepdims=True)
    fragv[...] = jnp.broadcast_to(frag_at, (8, HD))

    c_cp.wait()
    frag = jnp.broadcast_to(fragv[0:1, :], (128, HD))
    blocks = [Cl[:, j * HD:(j + 1) * HD].astype(F32) for j in range(6)]
    cut = blocks[0]
    for j in range(1, 6):
        cut = jnp.where(frag == float(j), blocks[j], cut)
    Cf[q] = cut.astype(BF16)
    for m in range(5):
        rest = jnp.where(frag <= float(m), blocks[m + 1], blocks[m]).astype(BF16)
        if m < NA:
            Ca[q, :, m * HD:(m + 1) * HD] = rest
        else:
            Cb[q, :, (m - NA) * HD:(m - NA + 1) * HD] = rest

    for cp in tok_cp:
        cp.wait()

    def rows(t, _):
        here = pl.ds(pl.multiple_of(t * 16, 16), 16)
        v = tok[here, :].astype(F32)
        m = jnp.sum(v * v, axis=-1, keepdims=True) * (1.0 / 8192)
        scale[here, :] = jnp.broadcast_to(lax.rsqrt(m + 1e-05), (16, 128))
        return 0

    lax.fori_loop(0, 8, rows, 0)

    def a_send(i, k):
        q2 = (q + k) % 8
        return pltpu.make_async_remote_copy(
            src_ref=S.at[i, q2], dst_ref=R.at[i, q], send_sem=a_s.at[i, k], recv_sem=a_r.at[i, k], device_id=dev(q2),
            device_id_type=MESH)

    def norm_chunk(i):
        def one(b, _):
            for h in range(2):
                col = pl.multiple_of(h * 4096 + b * 512 + i * 128, 128)
                v = tok[:, pl.ds(col, 128)].astype(F32)
                S[i, b, :, h * 128:(h + 1) * 128] = (v * scale[...] * gain[:, pl.ds(col, 128)]).astype(BF16)
            return 0

        lax.fori_loop(0, 8, one, 0)
        R[i, q] = S[i, q]

    def send_chunk(i):
        def one(k, _):
            a_send(i, k).start()
            return 0

        lax.fori_loop(1, 8, one, 0)

    def c_send(g, k):
        to = sib if k == 0 else dev(((y + k) % 4) * 2 + c)
        return pltpu.make_async_remote_copy(
            src_ref=C[g].at[q], dst_ref=C[g].at[q], send_sem=c_s.at[g, k], recv_sem=c_r.at[g, k], device_id=to,
            device_id_type=MESH)

    def c_pass(g, k):
        slot = ((y + 4 - k) % 4) * 2 + c
        return pltpu.make_async_remote_copy(
            src_ref=C[g].at[slot], dst_ref=C[g].at[slot], send_sem=f_s.at[g, k], recv_sem=f_r.at[g, k], device_id=sib,
            device_id_type=MESH)

    def spread(g):
        for k in (2, 1, 3, 0):
            c_send(g, k).start()

    def collect(g):
        for k in (1, 3, 2):
            c_send(g, k).wait_recv()
            c_pass(g, k).start()
        c_send(g, 0).wait_recv()
        for k in (1, 3, 2):
            c_pass(g, k).wait_recv()

    def w_send(i):
        return pltpu.make_async_remote_copy(
            src_ref=W2.at[i, xh], dst_ref=W2.at[i, xh], send_sem=w_s.at[i], recv_sem=w_r.at[i], device_id=xpart,
            device_id_type=MESH)

    norm_chunk(0)
    w_cp.wait()
    pl.semaphore_wait(bar, 39)

    spread(0)
    send_chunk(0)
    for i in range(NC):
        w_send(i).start()
    norm_chunk(1)
    send_chunk(1)
    norm_chunk(2)
    norm_chunk(3)
    collect(0)

    def g_send(g, i):
        return pltpu.make_async_remote_copy(
            src_ref=Gs[g].at[i], dst_ref=Gr[g].at[i], send_sem=g_s.at[g, i], recv_sem=g_r.at[g, i], device_id=xpart,
            device_id_type=MESH)

    def grads(g, i):
        lhs = R[i].reshape(1024, 256)
        width = C[g].shape[-1]
        for n in range(0, width, 256):
            cols = slice(n, min(n + 256, width))
            wide = cols.stop - cols.start
            d = lax.dot_general(
                lhs, C[g][:, :, cols].reshape(1024, wide), (((0,), (0,)), ((), ())), preferred_element_type=F32)
            Gt[g][i, :, :, cols] = d.reshape(2, 128, wide)
        Gs[g][i] = Gt[g][i, 1 - xh].astype(BF16)
        g_send(g, i).start()

    def x1_send(i, k):
        j = (((1 - i // 2) * 8 + (1 - i % 2) + 2 * (k // 2) + 11) % 16) * 2 + k % 2
        return j, pltpu.make_async_remote_copy(
            src_ref=D.at[i, k], dst_ref=X1.at[r], send_sem=x1_s, recv_sem=x1_r, device_id=(j, f), device_id_type=MESH)

    def offer(i):
        g_send(0, i).wait_recv()
        d = inner_rate * (Gtf[i, xh] + Grf[i].astype(F32))
        D[i] = d.astype(BF16).reshape(8, 16, HD)

        def one(k, _):
            j, cp = x1_send(i, k)

            @pl.when(j != r)
            def _():
                cp.start()

            @pl.when(j == r)
            def _():
                X1[r] = D[i, k]

            return 0

        lax.fori_loop(0, 8, one, 0)

    ring_at = (z + 5) % 16
    my_chunk = (1 - ring_at // 8) * 2 + (1 - ring_at % 2)
    my_piece = 2 * ((ring_at % 8) // 2) + r % 2

    def x2_send(k):
        d = (r + k) % 32
        return pltpu.make_async_remote_copy(
            src_ref=X2s.at[d], dst_ref=X2r.at[my_chunk, my_piece], send_sem=x2_s, recv_sem=x2_r.at[my_chunk],
            device_id=(d, f), device_id_type=MESH)

    def relay():
        whole = X1.at[pl.ds(0, 31)]
        pltpu.make_async_copy(whole, whole, x1_r).wait()

        def pick(d, _):
            X2s[d] = X1[partner[0, d]]
            return 0

        lax.fori_loop(0, 32, pick, 0)

        def one(k, _):
            x2_send(k).start()
            return 0

        lax.fori_loop(1, 32, one, 0)
        X2r[my_chunk, my_piece] = X2s[r]

    def step(t, _):
        def arrive(k, _):
            a_send(t, k).wait_recv()
            return 0

        lax.fori_loop(1, 8, arrive, 0)

        @pl.when(t == 0)
        def _():
            send_chunk(2)

        @pl.when(t == 1)
        def _():
            spread(1)
            send_chunk(3)

        grads(0, t)

        w_send(t).wait_recv()

        @pl.when(t == 0)
        def _():
            Pacc[...] = jnp.zeros_like(Pacc)

        lhs = R[t].reshape(1024, 256)
        for n in range(3):
            cols = slice(n * 256, (n + 1) * 256)
            p = jnp.dot(lhs, W2[t, :, :, cols].reshape(256, 256), preferred_element_type=F32)
            Pacc[:, :, cols] += p.reshape(8, 128, 256)

        @pl.when(t >= 1)
        def _():
            offer(t - 1)

        @pl.when(t == 2)
        def _():
            spread(2)
            collect(1)

            def early(i, _):
                grads(1, i)
                return 0

            lax.fori_loop(0, NC - 1, early, 0)

        return 0

    lax.fori_loop(0, NC, step, 0)

    p_send = pltpu.make_async_remote_copy(
        src_ref=Ps, dst_ref=Pr, send_sem=p_s, recv_sem=p_r, device_id=sib, device_id_type=MESH)
    for b in range(4):
        Ps[b] = Pacc[b * 2 + 1 - c].astype(BF16)
    p_send.start()
    offer(NC - 1)
    grads(1, NC - 1)

    @pl.when(my_chunk < 2)
    def _():
        relay()

    def k_send(k):
        y2 = (y + k) % 4
        return pltpu.make_async_remote_copy(
            src_ref=Ss.at[y2], dst_ref=Sr.at[k - 1], send_sem=k_s.at[k], recv_sem=k_r.at[k], device_id=dev(y2 * 2 + c),
            device_id_type=MESH)

    p_send.wait_recv()
    for k in (2, 1, 3):
        y2 = (y + k) % 4
        Ss[y2] = (Pacc[y2 * 2 + c] + Pr[y2].astype(F32)).astype(BF16)
        k_send(k).start()

    collect(2)

    def late(i, _):
        grads(2, i)
        return 0

    lax.fori_loop(0, NC, late, 0)

    @pl.when(my_chunk >= 2)
    def _():
        relay()

    for k in (1, 3, 2):
        k_send(k).wait_recv()
    own = Pacc[q] + Pr[y].astype(F32)
    keys_v[...] = (own + Sr[0].astype(F32) + Sr[1].astype(F32) + Sr[2].astype(F32)).astype(BF16)
    keys_cp = pltpu.make_async_copy(keys_v, keys_o, lsem.at[11])
    keys_cp.start()

    m_cp.wait()

    def add_up(i, _):
        g_send(1, i).wait_recv()
        g_send(2, i).wait_recv()
        Gta[i, xh] = Gta[i, xh] + Gra[i].astype(F32)
        Gtb[i, xh] = Gtb[i, xh] + Grb[i].astype(F32)
        return 0

    lax.fori_loop(0, NC, add_up, 0)

    def update(i, _):
        @pl.when(my_chunk == i)
        def _():
            part = X2r.at[i, pl.ds(0, 7)]
            pltpu.make_async_copy(part, part, x2_r.at[i]).wait()

        @pl.when(my_chunk != i)
        def _():
            part = X2r.at[i]
            pltpu.make_async_copy(part, part, x2_r.at[i]).wait()

        here = pl.ds(pl.multiple_of(i * 128, 128), 128)
        delta = D[i].reshape(128, HD).astype(F32)
        mix = (delta + X2r[i].reshape(128, HD).astype(F32)) * 0.5
        nm = beta_value * mom[here, :] + mix
        nm_v[here, :] = nm
        step_out = outer_rate * (beta_value * nm + mix)
        at = jnp.broadcast_to(fragv[0:1, :], (128, HD))

        def rest(m):
            if m < NA:
                return Gta[i, xh, :, m * HD:(m + 1) * HD]
            return Gtb[i, xh, :, (m - NA) * HD:(m - NA + 1) * HD]

        for j in range(6):
            cols = slice(j * HD, (j + 1) * HD)
            if j == 0:
                g = rest(0)
            elif j == 5:
                g = rest(4)
            else:
                g = jnp.where(at < float(j), rest(j - 1), rest(j))
            change = jnp.where(at == float(j), step_out, inner_rate * g)
            nw_v[here, cols] = (W2[i, xh, :, cols].astype(F32) - change).astype(BF16)
        return 0

    lax.fori_loop(0, NC, update, 0)
    nw_cp = pltpu.make_async_copy(nw_v, nw_o, lsem.at[12])
    nw_cp.start()
    nm_cp = pltpu.make_async_copy(nm_v, nm_o, lsem.at[13])
    nm_cp.start()

    for k in range(4):
        for g in range(3):
            c_send(g, k).wait_send()
            if k > 0:
                c_pass(g, k).wait_send()
        if k > 0:
            k_send(k).wait_send()
    p_send.wait_send()

    def sent(i, _):
        w_send(i).wait_send()
        for g in range(3):
            g_send(g, i).wait_send()

        def one(k, _):
            a_send(i, k).wait_send()
            return 0

        lax.fori_loop(1, 8, one, 0)
        return 0

    lax.fori_loop(0, NC, sent, 0)
    most = X1.at[pl.ds(0, 31)]
    pltpu.make_async_copy(most, most, x1_s).wait()
    pltpu.make_async_copy(most, most, x2_s).wait()
    for cp in (keys_cp, nw_cp, nm_cp):
        cp.wait()


def finish(keys, nw, nm, keys_o, nw_o, nm_o, keys_v, nw_v, nm_v, i_sem, o_sem):
    ways = [(nw.at[here], nw_v.at[here], nw_o.at[here]) for here in (pl.ds(0, 256), pl.ds(256, 256))]
    ways += [(nm, nm_v, nm_o), (keys, keys_v, keys_o)]
    into = [pltpu.make_async_copy(a, v, i_sem.at[n]) for n, (a, v, _) in enumerate(ways)]
    out = [pltpu.make_async_copy(v, b, o_sem.at[n]) for n, (_, v, b) in enumerate(ways)]
    for cp in into:
        cp.start()
    for cp, back in zip(into, out):
        cp.wait()
        back.start()
    for back in out:
        back.wait()


def body(tokens, norm_gain, weight, momentum, cotangent, fragment, partner):
    hbm = pl.BlockSpec(memory_space=pltpu.HBM)
    V = pltpu.VMEM
    dma = pltpu.SemaphoreType.DMA
    shapes = (
        jax.ShapeDtypeStruct((128, 768), BF16),
        jax.ShapeDtypeStruct((512, 768), BF16),
        jax.ShapeDtypeStruct((512, HD), F32),
    )
    na, nb = NA * HD, (5 - NA) * HD
    outs = pl.pallas_call(
        kernel,
        out_shape=shapes,
        in_specs=[hbm] * 7,
        out_specs=(hbm,) * 3,
        scratch_shapes=[
            V((128, 8192), BF16),
            V((128, 128), F32),
            V((NC, 8, 128, 256), BF16),
            V((NC, 8, 128, 256), BF16),
            V((NC, 2, 128, 768), BF16),
            V((128, 768), BF16),
            V((8, 128, HD), BF16), V((8, 128, na), BF16), V((8, 128, nb), BF16),
            V((NC, 2, 128, HD), F32), V((NC, 2, 128, na), F32), V((NC, 2, 128, nb), F32),
            V((NC, 128, HD), BF16), V((NC, 128, na), BF16), V((NC, 128, nb), BF16),
            V((NC, 128, HD), BF16), V((NC, 128, na), BF16), V((NC, 128, nb), BF16),
            V((8, 128, 768), F32),
            V((4, 128, 768), BF16),
            V((4, 128, 768), BF16),
            V((4, 128, 768), BF16),
            V((3, 128, 768), BF16),
            V((NC, 8, 16, HD), BF16),
            V((32, 16, HD), BF16),
            V((32, 16, HD), BF16),
            V((NC, 8, 16, HD), BF16),
            V((512, HD), F32),
            V((8, HD), F32),
            V((1, 8192), F32),
            V((1, 32), jnp.int32),
            V((1, 32), jnp.int32),
            pltpu.SMEM((1, 32), jnp.int32),
            V((128, 768), BF16), V((512, 768), BF16), V((512, HD), F32),
            dma((14,)),
            dma((NC, 8)), dma((NC, 8)),
            dma((NC,)), dma((NC,)),
            dma((3, 4)), dma((3, 4)),
            dma((3, 4)), dma((3, 4)),
            dma((3, NC)), dma((3, NC)),
            dma, dma,
            dma((4,)), dma((4,)),
            dma, dma,
            dma, dma((NC,)),
        ],
        compiler_params=pltpu.CompilerParams(
            collective_id=0, has_side_effects=True, vmem_limit_bytes=62 * 2**20
        ),
    )(tokens[0], norm_gain[None], weight[0].reshape(NC, 128, 768), momentum[0], cotangent[0], fragment[None], partner[None])
    keys, nw, nm = pl.pallas_call(
        finish,
        out_shape=shapes,
        in_specs=[hbm] * 3,
        out_specs=(hbm,) * 3,
        scratch_shapes=[V((128, 768), BF16), V((512, 768), BF16), V((512, HD), F32), dma((4,)), dma((4,))],
        compiler_params=pltpu.CompilerParams(vmem_limit_bytes=62 * 2**20),
    )(*outs)
    return (keys[None], nw[None], nm[None])


def solution(mesh):
    in_specs = (
        P("replica", "fsdp", None),
        P(),
        P("replica", "fsdp", None),
        P("replica", "fsdp", None),
        P("replica", "fsdp", None),
        P(),
        P(),
    )
    out_specs = (P("replica", "fsdp", None), P("replica", "fsdp", None), P("replica", "fsdp", None))
    return jax.shard_map(body, mesh=mesh, in_specs=in_specs, out_specs=out_specs, check_vma=False)
```

```python
import jax
import jax.numpy as jnp
from jax import lax
from jax.experimental import pallas as pl
from jax.experimental.pallas import tpu as pltpu
from jax.sharding import PartitionSpec as P

HD = 128
NC = 4
NA = 2
MESH = pl.DeviceIdType.MESH
F32 = jnp.float32
BF16 = jnp.bfloat16

inner_rate = 0.0001
outer_rate = 0.7
beta_value = 0.9


def kernel(
    tokens, gain_h, weight, momentum, cot, fragment_h, partner_h,
    keys_o, nw_o, nm_o,
    tok, scale, S, R, W2, Cl, Cf, Ca, Cb, Gtf, Gta, Gtb, Gsf, Gsa, Gsb, Grf, Gra, Grb, Pacc, Ps, Pr, Ss, Sr,
    D, X1, X2s, X2r, mom, fragv, gain, fragment, partner_row, partner, keys_v, nw_v, nm_v,
    lsem, a_s, a_r, w_s, w_r, c_s, c_r, f_s, f_r, g_s, g_r, p_s, p_r, k_s, k_r, x1_s, x1_r, x2_s, x2_r, near,
):
    r = lax.axis_index("replica")
    f = lax.axis_index("fsdp")
    xh = f // 8
    q = f % 8
    y = q // 2
    c = q % 2
    z = r // 2
    C = (Cf, Ca, Cb)
    Gt = (Gtf, Gta, Gtb)
    Gs = (Gsf, Gsa, Gsb)
    Gr = (Grf, Gra, Grb)

    def dev(q2):
        return (r, xh * 8 + q2)

    xpart = (r, (1 - xh) * 8 + q)
    sib = dev(y * 2 + 1 - c)

    small = [
        pltpu.make_async_copy(a, b, lsem.at[n])
        for n, (a, b) in enumerate(((fragment_h, fragment), (partner_h, partner_row), (partner_h, partner), (gain_h, gain)))
    ]
    c_cp = pltpu.make_async_copy(cot, Cl, lsem.at[4])
    w_cp = pltpu.make_async_copy(weight, W2.at[:, xh], lsem.at[5])
    m_cp = pltpu.make_async_copy(momentum, mom, lsem.at[6])
    tok_cp = [
        pltpu.make_async_copy(tokens.at[pl.ds(h * 32, 32)], tok.at[pl.ds(h * 32, 32)], lsem.at[7 + h])
        for h in range(4)
    ]
    for cp in [*small, c_cp, *tok_cp, w_cp, m_cp]:
        cp.start()

    bar = pltpu.get_barrier_semaphore()
    for k in range(1, 8):
        pl.semaphore_signal(bar, inc=1, device_id=dev((q + k) % 8), device_id_type=MESH)
    pl.semaphore_signal(bar, inc=1, device_id=xpart, device_id_type=MESH)

    pl.semaphore_signal(bar, inc=1, device_id=(z * 2 + 1 - r % 2, f), device_id_type=MESH)

    def in_line(away):
        return (z + away >= 0) & (z + away < 16)

    for away in (-1, 1):
        @pl.when(in_line(away))
        def _():
            for h in range(2):
                pl.semaphore_signal(bar, inc=1, device_id=((z + away) * 2 + h, f), device_id_type=MESH)

    def tell(level):
        far = 2 ** level
        for away in (-far, far):
            @pl.when(in_line(away))
            def _():
                pl.semaphore_signal(near.at[level], inc=1, device_id=(r + 2 * away, f), device_id_type=MESH)

    def hear(level):
        far = 2 ** level
        pl.semaphore_wait(near.at[level], jnp.minimum(z // far, 1) + jnp.minimum((15 - z) // far, 1))

    for cp in small:
        cp.wait()
    lane = lax.broadcasted_iota(jnp.int32, (8, 32), 1).astype(F32)
    mine = r.astype(F32)
    partners = jnp.broadcast_to(partner_row[...].astype(F32), (8, 32))
    mate = jnp.sum(jnp.where(lane == mine, partners, 0.0), axis=-1, keepdims=True)
    fragments = jnp.broadcast_to(fragment[...].astype(F32), (8, 32))
    frag_at = jnp.sum(jnp.where(lane == jnp.minimum(mate, mine), fragments, 0.0), axis=-1, keepdims=True)
    fragv[...] = jnp.broadcast_to(frag_at, (8, HD))

    c_cp.wait()
    frag = jnp.broadcast_to(fragv[0:1, :], (128, HD))
    blocks = [Cl[:, j * HD:(j + 1) * HD].astype(F32) for j in range(6)]
    cut = blocks[0]
    for j in range(1, 6):
        cut = jnp.where(frag == float(j), blocks[j], cut)
    Cf[q] = cut.astype(BF16)
    for m in range(5):
        rest = jnp.where(frag <= float(m), blocks[m + 1], blocks[m]).astype(BF16)
        if m < NA:
            Ca[q, :, m * HD:(m + 1) * HD] = rest
        else:
            Cb[q, :, (m - NA) * HD:(m - NA + 1) * HD] = rest

    for cp in tok_cp:
        cp.wait()

    def rows(t, _):
        here = pl.ds(pl.multiple_of(t * 16, 16), 16)
        v = tok[here, :].astype(F32)
        m = jnp.sum(v * v, axis=-1, keepdims=True) * (1.0 / 8192)
        scale[here, :] = jnp.broadcast_to(lax.rsqrt(m + 1e-05), (16, 128))
        return 0

    lax.fori_loop(0, 8, rows, 0)

    def a_send(i, k):
        q2 = (q + k) % 8
        return pltpu.make_async_remote_copy(
            src_ref=S.at[i, q2], dst_ref=R.at[i, q], send_sem=a_s.at[i, k], recv_sem=a_r.at[i, k], device_id=dev(q2),
            device_id_type=MESH)

    def norm_chunk(i):
        def one(b, _):
            for h in range(2):
                col = pl.multiple_of(h * 4096 + b * 512 + i * 128, 128)
                v = tok[:, pl.ds(col, 128)].astype(F32)
                S[i, b, :, h * 128:(h + 1) * 128] = (v * scale[...] * gain[:, pl.ds(col, 128)]).astype(BF16)
            return 0

        lax.fori_loop(0, 8, one, 0)
        R[i, q] = S[i, q]

    def send_chunk(i):
        def one(k, _):
            a_send(i, k).start()
            return 0

        lax.fori_loop(1, 8, one, 0)

    def c_send(g, k):
        to = sib if k == 0 else dev(((y + k) % 4) * 2 + c)
        return pltpu.make_async_remote_copy(
            src_ref=C[g].at[q], dst_ref=C[g].at[q], send_sem=c_s.at[g, k], recv_sem=c_r.at[g, k], device_id=to,
            device_id_type=MESH)

    def c_pass(g, k):
        slot = ((y + 4 - k) % 4) * 2 + c
        return pltpu.make_async_remote_copy(
            src_ref=C[g].at[slot], dst_ref=C[g].at[slot], send_sem=f_s.at[g, k], recv_sem=f_r.at[g, k], device_id=sib,
            device_id_type=MESH)

    def spread(g):
        for k in (2, 1, 3, 0):
            c_send(g, k).start()

    def collect(g):
        for k in (1, 3, 2):
            c_send(g, k).wait_recv()
            c_pass(g, k).start()
        c_send(g, 0).wait_recv()
        for k in (1, 3, 2):
            c_pass(g, k).wait_recv()

    def w_send(i):
        return pltpu.make_async_remote_copy(
            src_ref=W2.at[i, xh], dst_ref=W2.at[i, xh], send_sem=w_s.at[i], recv_sem=w_r.at[i], device_id=xpart,
            device_id_type=MESH)

    norm_chunk(0)
    w_cp.wait()
    pl.semaphore_wait(bar, 9 + 2 * jnp.minimum(z, 1) + 2 * jnp.minimum(15 - z, 1))

    spread(0)
    send_chunk(0)
    for i in range(NC):
        w_send(i).start()
    norm_chunk(1)
    send_chunk(1)
    tell(0)
    norm_chunk(2)
    norm_chunk(3)
    collect(0)
    hear(0)
    tell(1)

    def g_send(g, i):
        return pltpu.make_async_remote_copy(
            src_ref=Gs[g].at[i], dst_ref=Gr[g].at[i], send_sem=g_s.at[g, i], recv_sem=g_r.at[g, i], device_id=xpart,
            device_id_type=MESH)

    def grads(g, i):
        lhs = R[i].reshape(1024, 256)
        width = C[g].shape[-1]
        for n in range(0, width, 256):
            cols = slice(n, min(n + 256, width))
            wide = cols.stop - cols.start
            d = lax.dot_general(
                lhs, C[g][:, :, cols].reshape(1024, wide), (((0,), (0,)), ((), ())), preferred_element_type=F32)
            Gt[g][i, :, :, cols] = d.reshape(2, 128, wide)
        Gs[g][i] = Gt[g][i, 1 - xh].astype(BF16)
        g_send(g, i).start()

    def x1_send(i, k):
        j = (((1 - i // 2) * 8 + (1 - i % 2) + 2 * (k // 2) + 11) % 16) * 2 + k % 2
        return j, pltpu.make_async_remote_copy(
            src_ref=D.at[i, k], dst_ref=X1.at[r], send_sem=x1_s, recv_sem=x1_r, device_id=(j, f), device_id_type=MESH)

    def offer(i):
        g_send(0, i).wait_recv()
        d = inner_rate * (Gtf[i, xh] + Grf[i].astype(F32))
        D[i] = d.astype(BF16).reshape(8, 16, HD)

        def one(k, _):
            j, cp = x1_send(i, k)

            @pl.when(j != r)
            def _():
                cp.start()

            @pl.when(j == r)
            def _():
                X1[r] = D[i, k]

            return 0

        lax.fori_loop(0, 8, one, 0)

    ring_at = (z + 5) % 16
    my_chunk = (1 - ring_at // 8) * 2 + (1 - ring_at % 2)
    my_piece = 2 * ((ring_at % 8) // 2) + r % 2

    def x2_send(k):
        d = (r + k) % 32
        return pltpu.make_async_remote_copy(
            src_ref=X2s.at[d], dst_ref=X2r.at[my_chunk, my_piece], send_sem=x2_s, recv_sem=x2_r.at[my_chunk],
            device_id=(d, f), device_id_type=MESH)

    def relay():
        whole = X1.at[pl.ds(0, 31)]
        pltpu.make_async_copy(whole, whole, x1_r).wait()

        def pick(d, _):
            X2s[d] = X1[partner[0, d]]
            return 0

        lax.fori_loop(0, 32, pick, 0)

        def one(k, _):
            x2_send(k).start()
            return 0

        lax.fori_loop(1, 32, one, 0)
        X2r[my_chunk, my_piece] = X2s[r]

    def step(t, _):
        def arrive(k, _):
            a_send(t, k).wait_recv()
            return 0

        lax.fori_loop(1, 8, arrive, 0)

        @pl.when(t == 0)
        def _():
            spread(1)
            send_chunk(2)

        @pl.when(t == 1)
        def _():
            send_chunk(3)

        grads(0, t)

        w_send(t).wait_recv()

        @pl.when(t == 0)
        def _():
            Pacc[...] = jnp.zeros_like(Pacc)

        lhs = R[t].reshape(1024, 256)
        for n in range(3):
            cols = slice(n * 256, (n + 1) * 256)
            p = jnp.dot(lhs, W2[t, :, :, cols].reshape(256, 256), preferred_element_type=F32)
            Pacc[:, :, cols] += p.reshape(8, 128, 256)

        @pl.when(t == 0)
        def _():
            hear(1)
            tell(2)

        @pl.when(t == 1)
        def _():
            hear(2)
            tell(3)

        @pl.when(t == 2)
        def _():
            spread(2)
            collect(1)

            def early(i, _):
                grads(1, i)
                return 0

            lax.fori_loop(0, NC - 1, early, 0)

        return 0

    lax.fori_loop(0, NC, step, 0)

    p_send = pltpu.make_async_remote_copy(
        src_ref=Ps, dst_ref=Pr, send_sem=p_s, recv_sem=p_r, device_id=sib, device_id_type=MESH)
    for b in range(4):
        Ps[b] = Pacc[b * 2 + 1 - c].astype(BF16)
    p_send.start()
    hear(3)

    def offers(i, _):
        offer(i)
        return 0

    lax.fori_loop(0, NC, offers, 0)
    grads(1, NC - 1)

    @pl.when(my_chunk < 2)
    def _():
        relay()

    def k_send(k):
        y2 = (y + k) % 4
        return pltpu.make_async_remote_copy(
            src_ref=Ss.at[y2], dst_ref=Sr.at[k - 1], send_sem=k_s.at[k], recv_sem=k_r.at[k], device_id=dev(y2 * 2 + c),
            device_id_type=MESH)

    p_send.wait_recv()
    for k in (2, 1, 3):
        y2 = (y + k) % 4
        Ss[y2] = (Pacc[y2 * 2 + c] + Pr[y2].astype(F32)).astype(BF16)
        k_send(k).start()

    collect(2)

    def late(i, _):
        grads(2, i)
        return 0

    lax.fori_loop(0, NC, late, 0)

    @pl.when(my_chunk >= 2)
    def _():
        relay()

    for k in (1, 3, 2):
        k_send(k).wait_recv()
    own = Pacc[q] + Pr[y].astype(F32)
    keys_v[...] = (own + Sr[0].astype(F32) + Sr[1].astype(F32) + Sr[2].astype(F32)).astype(BF16)
    keys_cp = pltpu.make_async_copy(keys_v, keys_o, lsem.at[11])
    keys_cp.start()

    m_cp.wait()

    def add_up(i, _):
        g_send(1, i).wait_recv()
        g_send(2, i).wait_recv()
        Gta[i, xh] = Gta[i, xh] + Gra[i].astype(F32)
        Gtb[i, xh] = Gtb[i, xh] + Grb[i].astype(F32)
        return 0

    lax.fori_loop(0, NC, add_up, 0)

    def update(i, _):
        @pl.when(my_chunk == i)
        def _():
            part = X2r.at[i, pl.ds(0, 7)]
            pltpu.make_async_copy(part, part, x2_r.at[i]).wait()

        @pl.when(my_chunk != i)
        def _():
            part = X2r.at[i]
            pltpu.make_async_copy(part, part, x2_r.at[i]).wait()

        here = pl.ds(pl.multiple_of(i * 128, 128), 128)
        delta = D[i].reshape(128, HD).astype(F32)
        mix = (delta + X2r[i].reshape(128, HD).astype(F32)) * 0.5
        nm = beta_value * mom[here, :] + mix
        nm_v[here, :] = nm
        step_out = outer_rate * (beta_value * nm + mix)
        at = jnp.broadcast_to(fragv[0:1, :], (128, HD))

        def rest(m):
            if m < NA:
                return Gta[i, xh, :, m * HD:(m + 1) * HD]
            return Gtb[i, xh, :, (m - NA) * HD:(m - NA + 1) * HD]

        for j in range(6):
            cols = slice(j * HD, (j + 1) * HD)
            if j == 0:
                g = rest(0)
            elif j == 5:
                g = rest(4)
            else:
                g = jnp.where(at < float(j), rest(j - 1), rest(j))
            change = jnp.where(at == float(j), step_out, inner_rate * g)
            nw_v[here, cols] = (W2[i, xh, :, cols].astype(F32) - change).astype(BF16)
        return 0

    lax.fori_loop(0, NC, update, 0)
    nw_cp = pltpu.make_async_copy(nw_v, nw_o, lsem.at[12])
    nw_cp.start()
    nm_cp = pltpu.make_async_copy(nm_v, nm_o, lsem.at[13])
    nm_cp.start()

    for k in range(4):
        for g in range(3):
            c_send(g, k).wait_send()
            if k > 0:
                c_pass(g, k).wait_send()
        if k > 0:
            k_send(k).wait_send()
    p_send.wait_send()

    def sent(i, _):
        w_send(i).wait_send()
        for g in range(3):
            g_send(g, i).wait_send()

        def one(k, _):
            a_send(i, k).wait_send()
            return 0

        lax.fori_loop(1, 8, one, 0)
        return 0

    lax.fori_loop(0, NC, sent, 0)
    most = X1.at[pl.ds(0, 31)]
    pltpu.make_async_copy(most, most, x1_s).wait()
    pltpu.make_async_copy(most, most, x2_s).wait()
    for cp in (keys_cp, nw_cp, nm_cp):
        cp.wait()


def finish(keys, nw, nm, keys_o, nw_o, nm_o, keys_v, nw_v, nm_v, i_sem, o_sem):
    ways = [(nw.at[here], nw_v.at[here], nw_o.at[here]) for here in (pl.ds(0, 256), pl.ds(256, 256))]
    ways += [(nm, nm_v, nm_o), (keys, keys_v, keys_o)]
    into = [pltpu.make_async_copy(a, v, i_sem.at[n]) for n, (a, v, _) in enumerate(ways)]
    out = [pltpu.make_async_copy(v, b, o_sem.at[n]) for n, (_, v, b) in enumerate(ways)]
    for cp in into:
        cp.start()
    for cp, back in zip(into, out):
        cp.wait()
        back.start()
    for back in out:
        back.wait()


def body(tokens, norm_gain, weight, momentum, cotangent, fragment, partner):
    hbm = pl.BlockSpec(memory_space=pltpu.HBM)
    V = pltpu.VMEM
    dma = pltpu.SemaphoreType.DMA
    shapes = (
        jax.ShapeDtypeStruct((128, 768), BF16),
        jax.ShapeDtypeStruct((512, 768), BF16),
        jax.ShapeDtypeStruct((512, HD), F32),
    )
    na, nb = NA * HD, (5 - NA) * HD
    outs = pl.pallas_call(
        kernel,
        out_shape=shapes,
        in_specs=[hbm] * 7,
        out_specs=(hbm,) * 3,
        scratch_shapes=[
            V((128, 8192), BF16),
            V((128, 128), F32),
            V((NC, 8, 128, 256), BF16),
            V((NC, 8, 128, 256), BF16),
            V((NC, 2, 128, 768), BF16),
            V((128, 768), BF16),
            V((8, 128, HD), BF16), V((8, 128, na), BF16), V((8, 128, nb), BF16),
            V((NC, 2, 128, HD), F32), V((NC, 2, 128, na), F32), V((NC, 2, 128, nb), F32),
            V((NC, 128, HD), BF16), V((NC, 128, na), BF16), V((NC, 128, nb), BF16),
            V((NC, 128, HD), BF16), V((NC, 128, na), BF16), V((NC, 128, nb), BF16),
            V((8, 128, 768), F32),
            V((4, 128, 768), BF16),
            V((4, 128, 768), BF16),
            V((4, 128, 768), BF16),
            V((3, 128, 768), BF16),
            V((NC, 8, 16, HD), BF16),
            V((32, 16, HD), BF16),
            V((32, 16, HD), BF16),
            V((NC, 8, 16, HD), BF16),
            V((512, HD), F32),
            V((8, HD), F32),
            V((1, 8192), F32),
            V((1, 32), jnp.int32),
            V((1, 32), jnp.int32),
            pltpu.SMEM((1, 32), jnp.int32),
            V((128, 768), BF16), V((512, 768), BF16), V((512, HD), F32),
            dma((14,)),
            dma((NC, 8)), dma((NC, 8)),
            dma((NC,)), dma((NC,)),
            dma((3, 4)), dma((3, 4)),
            dma((3, 4)), dma((3, 4)),
            dma((3, NC)), dma((3, NC)),
            dma, dma,
            dma((4,)), dma((4,)),
            dma, dma,
            dma, dma((NC,)),
            pltpu.SemaphoreType.REGULAR((4,)),
        ],
        compiler_params=pltpu.CompilerParams(
            collective_id=0, has_side_effects=True, vmem_limit_bytes=62 * 2**20
        ),
    )(tokens[0], norm_gain[None], weight[0].reshape(NC, 128, 768), momentum[0], cotangent[0], fragment[None], partner[None])
    keys, nw, nm = pl.pallas_call(
        finish,
        out_shape=shapes,
        in_specs=[hbm] * 3,
        out_specs=(hbm,) * 3,
        scratch_shapes=[V((128, 768), BF16), V((512, 768), BF16), V((512, HD), F32), dma((4,)), dma((4,))],
        compiler_params=pltpu.CompilerParams(vmem_limit_bytes=62 * 2**20),
    )(*outs)
    return (keys[None], nw[None], nm[None])


def solution(mesh):
    in_specs = (
        P("replica", "fsdp", None),
        P(),
        P("replica", "fsdp", None),
        P("replica", "fsdp", None),
        P("replica", "fsdp", None),
        P(),
        P(),
    )
    out_specs = (P("replica", "fsdp", None), P("replica", "fsdp", None), P("replica", "fsdp", None))
    return jax.shard_map(body, mesh=mesh, in_specs=in_specs, out_specs=out_specs, check_vma=False)
```

```python
import jax
import jax.numpy as jnp
from jax import lax
from jax.experimental import pallas as pl
from jax.experimental.pallas import tpu as pltpu
from jax.sharding import PartitionSpec as P

HD = 128
NC = 4
NA = 2
MESH = pl.DeviceIdType.MESH
F32 = jnp.float32
BF16 = jnp.bfloat16

inner_rate = 0.0001
outer_rate = 0.7
beta_value = 0.9


def kernel(
    tokens, gain_h, weight, momentum, cot, fragment_h, partner_h,
    keys_o, nw_o, nm_o,
    tok, scale, S, R, W2, Cl, Cf, Ca, Cb, Gtf, Gta, Gtb, Gsf, Gsa, Gsb, Grf, Gra, Grb, Pacc, Ps, Pr, Ss, Sr,
    D, X1, X2s, X2r, mom, fragv, gain, fragment, partner_row, partner, keys_v, nw_v, nm_v,
    lsem, a_s, a_r, w_s, w_r, c_s, c_r, f_s, f_r, g_s, g_r, p_s, p_r, k_s, k_r, x1_s, x1_r, x2_s, x2_r, near, o_sem,
):
    r = lax.axis_index("replica")
    f = lax.axis_index("fsdp")
    xh = f // 8
    q = f % 8
    y = q // 2
    c = q % 2
    z = r // 2
    C = (Cf, Ca, Cb)
    Gt = (Gtf, Gta, Gtb)
    Gs = (Gsf, Gsa, Gsb)
    Gr = (Grf, Gra, Grb)

    def dev(q2):
        return (r, xh * 8 + q2)

    xpart = (r, (1 - xh) * 8 + q)
    sib = dev(y * 2 + 1 - c)

    small = [
        pltpu.make_async_copy(a, b, lsem.at[n])
        for n, (a, b) in enumerate(((fragment_h, fragment), (partner_h, partner_row), (partner_h, partner), (gain_h, gain)))
    ]
    c_cp = pltpu.make_async_copy(cot, Cl, lsem.at[4])
    w_cp = pltpu.make_async_copy(weight, W2.at[:, xh], lsem.at[5])
    m_cp = pltpu.make_async_copy(momentum, mom, lsem.at[6])
    tok_cp = [
        pltpu.make_async_copy(tokens.at[pl.ds(h * 32, 32)], tok.at[pl.ds(h * 32, 32)], lsem.at[7 + h])
        for h in range(4)
    ]
    for cp in [*small, c_cp, *tok_cp, w_cp, m_cp]:
        cp.start()

    bar = pltpu.get_barrier_semaphore()
    for k in range(1, 8):
        pl.semaphore_signal(bar, inc=1, device_id=dev((q + k) % 8), device_id_type=MESH)
    pl.semaphore_signal(bar, inc=1, device_id=xpart, device_id_type=MESH)

    pl.semaphore_signal(bar, inc=1, device_id=(z * 2 + 1 - r % 2, f), device_id_type=MESH)

    def in_line(away):
        return (z + away >= 0) & (z + away < 16)

    for away in (-1, 1):
        @pl.when(in_line(away))
        def _():
            for h in range(2):
                pl.semaphore_signal(bar, inc=1, device_id=((z + away) * 2 + h, f), device_id_type=MESH)

    def tell(level):
        far = 2 ** level
        for away in (-far, far):
            @pl.when(in_line(away))
            def _():
                pl.semaphore_signal(near.at[level], inc=1, device_id=(r + 2 * away, f), device_id_type=MESH)

    def hear(level):
        far = 2 ** level
        pl.semaphore_wait(near.at[level], jnp.minimum(z // far, 1) + jnp.minimum((15 - z) // far, 1))

    for cp in small:
        cp.wait()
    lane = lax.broadcasted_iota(jnp.int32, (8, 32), 1).astype(F32)
    mine = r.astype(F32)
    partners = jnp.broadcast_to(partner_row[...].astype(F32), (8, 32))
    mate = jnp.sum(jnp.where(lane == mine, partners, 0.0), axis=-1, keepdims=True)
    fragments = jnp.broadcast_to(fragment[...].astype(F32), (8, 32))
    frag_at = jnp.sum(jnp.where(lane == jnp.minimum(mate, mine), fragments, 0.0), axis=-1, keepdims=True)
    fragv[...] = jnp.broadcast_to(frag_at, (8, HD))

    c_cp.wait()
    frag = jnp.broadcast_to(fragv[0:1, :], (128, HD))
    blocks = [Cl[:, j * HD:(j + 1) * HD].astype(F32) for j in range(6)]
    cut = blocks[0]
    for j in range(1, 6):
        cut = jnp.where(frag == float(j), blocks[j], cut)
    Cf[q] = cut.astype(BF16)
    for m in range(5):
        rest = jnp.where(frag <= float(m), blocks[m + 1], blocks[m]).astype(BF16)
        if m < NA:
            Ca[q, :, m * HD:(m + 1) * HD] = rest
        else:
            Cb[q, :, (m - NA) * HD:(m - NA + 1) * HD] = rest

    def rows(t, _):
        here = pl.ds(pl.multiple_of(t * 16, 16), 16)
        v = tok[here, :].astype(F32)
        m = jnp.sum(v * v, axis=-1, keepdims=True) * (1.0 / 8192)
        scale[here, :] = jnp.broadcast_to(lax.rsqrt(m + 1e-05), (16, 128))
        return 0

    for h, cp in enumerate(tok_cp):
        cp.wait()
        lax.fori_loop(2 * h, 2 * h + 2, rows, 0)

    def a_send(i, k):
        q2 = (q + k) % 8
        return pltpu.make_async_remote_copy(
            src_ref=S.at[i, q2], dst_ref=R.at[i, q], send_sem=a_s.at[i, k], recv_sem=a_r.at[i, k], device_id=dev(q2),
            device_id_type=MESH)

    def norm_chunk(i):
        def one(b, _):
            for h in range(2):
                col = pl.multiple_of(h * 4096 + b * 512 + i * 128, 128)
                v = tok[:, pl.ds(col, 128)].astype(F32)
                S[i, b, :, h * 128:(h + 1) * 128] = (v * scale[...] * gain[:, pl.ds(col, 128)]).astype(BF16)
            return 0

        lax.fori_loop(0, 8, one, 0)
        R[i, q] = S[i, q]

    def send_chunk(i):
        def one(k, _):
            a_send(i, k).start()
            return 0

        lax.fori_loop(1, 8, one, 0)

    def c_send(g, k):
        to = sib if k == 0 else dev(((y + k) % 4) * 2 + c)
        return pltpu.make_async_remote_copy(
            src_ref=C[g].at[q], dst_ref=C[g].at[q], send_sem=c_s.at[g, k], recv_sem=c_r.at[g, k], device_id=to,
            device_id_type=MESH)

    def c_pass(g, k):
        slot = ((y + 4 - k) % 4) * 2 + c
        return pltpu.make_async_remote_copy(
            src_ref=C[g].at[slot], dst_ref=C[g].at[slot], send_sem=f_s.at[g, k], recv_sem=f_r.at[g, k], device_id=sib,
            device_id_type=MESH)

    def spread(g):
        for k in (2, 1, 3, 0):
            c_send(g, k).start()

    def collect(g):
        for k in (1, 3, 2):
            c_send(g, k).wait_recv()
            c_pass(g, k).start()
        c_send(g, 0).wait_recv()
        for k in (1, 3, 2):
            c_pass(g, k).wait_recv()

    def w_send(i):
        return pltpu.make_async_remote_copy(
            src_ref=W2.at[i, xh], dst_ref=W2.at[i, xh], send_sem=w_s.at[i], recv_sem=w_r.at[i], device_id=xpart,
            device_id_type=MESH)

    norm_chunk(0)
    w_cp.wait()
    pl.semaphore_wait(bar, 9 + 2 * jnp.minimum(z, 1) + 2 * jnp.minimum(15 - z, 1))

    spread(0)
    send_chunk(0)
    for i in range(NC):
        w_send(i).start()
    norm_chunk(1)
    send_chunk(1)
    tell(0)
    norm_chunk(2)
    norm_chunk(3)
    collect(0)
    hear(0)
    tell(1)

    def g_send(g, i):
        return pltpu.make_async_remote_copy(
            src_ref=Gs[g].at[i], dst_ref=Gr[g].at[i], send_sem=g_s.at[g, i], recv_sem=g_r.at[g, i], device_id=xpart,
            device_id_type=MESH)

    def grads(g, i):
        lhs = R[i].reshape(1024, 256)
        width = C[g].shape[-1]
        for n in range(0, width, 256):
            cols = slice(n, min(n + 256, width))
            wide = cols.stop - cols.start
            d = lax.dot_general(
                lhs, C[g][:, :, cols].reshape(1024, wide), (((0,), (0,)), ((), ())), preferred_element_type=F32)
            Gt[g][i, :, :, cols] = d.reshape(2, 128, wide)
        Gs[g][i] = Gt[g][i, 1 - xh].astype(BF16)
        g_send(g, i).start()

    def x1_send(i, k):
        j = (((1 - i // 2) * 8 + (1 - i % 2) + 2 * (k // 2) + 11) % 16) * 2 + k % 2
        return j, pltpu.make_async_remote_copy(
            src_ref=D.at[i, k], dst_ref=X1.at[r], send_sem=x1_s, recv_sem=x1_r, device_id=(j, f), device_id_type=MESH)

    def offer(i):
        g_send(0, i).wait_recv()
        d = inner_rate * (Gtf[i, xh] + Grf[i].astype(F32))
        D[i] = d.astype(BF16).reshape(8, 16, HD)

        def one(k, _):
            j, cp = x1_send(i, k)

            @pl.when(j != r)
            def _():
                cp.start()

            @pl.when(j == r)
            def _():
                X1[r] = D[i, k]

            return 0

        lax.fori_loop(0, 8, one, 0)

    def offers(first, last):
        def one(i, _):
            offer(i)
            return 0

        lax.fori_loop(first, last, one, 0)

    ring_at = (z + 5) % 16
    my_chunk = (1 - ring_at // 8) * 2 + (1 - ring_at % 2)
    my_piece = 2 * ((ring_at % 8) // 2) + r % 2

    def x2_send(d):
        return pltpu.make_async_remote_copy(
            src_ref=X2s.at[d], dst_ref=X2r.at[my_chunk, my_piece], send_sem=x2_s, recv_sem=x2_r.at[my_chunk],
            device_id=(d, f), device_id_type=MESH)

    def relay():
        whole = X1.at[pl.ds(0, 31)]
        pltpu.make_async_copy(whole, whole, x1_r).wait()

        def one(d, _):
            X2s[d] = X1[partner[0, d]]

            @pl.when(d != r)
            def _():
                x2_send(d).start()

            return 0

        lax.fori_loop(0, 32, one, 0)
        X2r[my_chunk, my_piece] = X2s[r]

    def step(t, _):
        def arrive(k, _):
            a_send(t, k).wait_recv()
            return 0

        lax.fori_loop(1, 8, arrive, 0)

        @pl.when(t == 0)
        def _():
            spread(1)
            send_chunk(2)

        @pl.when(t == 1)
        def _():
            send_chunk(3)

        grads(0, t)

        w_send(t).wait_recv()

        @pl.when(t == 0)
        def _():
            Pacc[...] = jnp.zeros_like(Pacc)

        lhs = R[t].reshape(1024, 256)
        for n in range(3):
            cols = slice(n * 256, (n + 1) * 256)
            p = jnp.dot(lhs, W2[t, :, :, cols].reshape(256, 256), preferred_element_type=F32)
            Pacc[:, :, cols] += p.reshape(8, 128, 256)

        @pl.when(t == 0)
        def _():
            hear(1)
            tell(2)

        @pl.when(t == 1)
        def _():
            hear(2)
            tell(3)

        @pl.when(t == 2)
        def _():
            spread(2)
            collect(1)

            def early(i, _):
                grads(1, i)
                return 0

            lax.fori_loop(0, NC - 1, early, 0)
            hear(3)
            offers(0, NC - 2)

        return 0

    lax.fori_loop(0, NC, step, 0)

    p_send = pltpu.make_async_remote_copy(
        src_ref=Ps, dst_ref=Pr, send_sem=p_s, recv_sem=p_r, device_id=sib, device_id_type=MESH)
    for b in range(4):
        Ps[b] = Pacc[b * 2 + 1 - c].astype(BF16)
    p_send.start()
    offers(NC - 2, NC)
    grads(1, NC - 1)

    def k_send(k):
        y2 = (y + k) % 4
        return pltpu.make_async_remote_copy(
            src_ref=Ss.at[y2], dst_ref=Sr.at[k - 1], send_sem=k_s.at[k], recv_sem=k_r.at[k], device_id=dev(y2 * 2 + c),
            device_id_type=MESH)

    p_send.wait_recv()
    for k in (2, 1, 3):
        y2 = (y + k) % 4
        Ss[y2] = (Pacc[y2 * 2 + c] + Pr[y2].astype(F32)).astype(BF16)
        k_send(k).start()

    collect(2)

    def late(i, _):
        grads(2, i)
        return 0

    lax.fori_loop(0, NC, late, 0)

    relay()

    for k in (1, 3, 2):
        k_send(k).wait_recv()
    own = Pacc[q] + Pr[y].astype(F32)
    keys_v[...] = (own + Sr[0].astype(F32) + Sr[1].astype(F32) + Sr[2].astype(F32)).astype(BF16)
    keys_cp = pltpu.make_async_copy(keys_v, keys_o, lsem.at[11])
    keys_cp.start()

    m_cp.wait()

    def inner(i, _):
        g_send(1, i).wait_recv()
        g_send(2, i).wait_recv()
        here = pl.ds(pl.multiple_of(i * 128, 128), 128)
        at = jnp.broadcast_to(fragv[0:1, :], (128, HD))

        def rest(m):
            g, n = (1, m) if m < NA else (2, m - NA)
            cols = slice(n * HD, (n + 1) * HD)
            return Gt[g][i, xh, :, cols] + Gr[g][i, :, cols].astype(F32)

        grads_of = [rest(m) for m in range(5)]
        for j in range(6):
            if j == 0:
                g = grads_of[0]
            elif j == 5:
                g = grads_of[4]
            else:
                g = jnp.where(at < float(j), grads_of[j - 1], grads_of[j])
            cols = slice(j * HD, (j + 1) * HD)
            nw_v[here, cols] = (W2[i, xh, :, cols].astype(F32) - inner_rate * g).astype(BF16)
        return 0

    lax.fori_loop(0, NC, inner, 0)

    def out_copies(i):
        here = pl.ds(pl.multiple_of(i * 128, 128), 128)
        return (
            pltpu.make_async_copy(nw_v.at[here], nw_o.at[here], o_sem.at[0, i]),
            pltpu.make_async_copy(nm_v.at[here], nm_o.at[here], o_sem.at[1, i]),
        )

    def update(i, _):
        @pl.when(my_chunk == i)
        def _():
            part = X2r.at[i, pl.ds(0, 7)]
            pltpu.make_async_copy(part, part, x2_r.at[i]).wait()

        @pl.when(my_chunk != i)
        def _():
            part = X2r.at[i]
            pltpu.make_async_copy(part, part, x2_r.at[i]).wait()

        here = pl.ds(pl.multiple_of(i * 128, 128), 128)
        delta = D[i].reshape(128, HD).astype(F32)
        mix = (delta + X2r[i].reshape(128, HD).astype(F32)) * 0.5
        nm = beta_value * mom[here, :] + mix
        nm_v[here, :] = nm
        step_out = outer_rate * (beta_value * nm + mix)
        at = jnp.broadcast_to(fragv[0:1, :], (128, HD))
        for j in range(6):
            cols = slice(j * HD, (j + 1) * HD)
            outer = W2[i, xh, :, cols].astype(F32) - step_out
            nw_v[here, cols] = jnp.where(at == float(j), outer, nw_v[here, cols].astype(F32)).astype(BF16)
        for cp in out_copies(i):
            cp.start()
        return 0

    lax.fori_loop(0, NC, update, 0)

    for k in range(4):
        for g in range(3):
            c_send(g, k).wait_send()
            if k > 0:
                c_pass(g, k).wait_send()
        if k > 0:
            k_send(k).wait_send()
    p_send.wait_send()

    def sent(i, _):
        w_send(i).wait_send()
        for g in range(3):
            g_send(g, i).wait_send()

        def one(k, _):
            a_send(i, k).wait_send()
            return 0

        lax.fori_loop(1, 8, one, 0)
        return 0

    lax.fori_loop(0, NC, sent, 0)
    most = X1.at[pl.ds(0, 31)]
    pltpu.make_async_copy(most, most, x1_s).wait()
    pltpu.make_async_copy(most, most, x2_s).wait()
    keys_cp.wait()

    def written(i, _):
        for cp in out_copies(i):
            cp.wait()
        return 0

    lax.fori_loop(0, NC, written, 0)


def finish(keys, nw, nm, keys_o, nw_o, nm_o, keys_v, nw_v, nm_v, i_sem, o_sem):
    ways = [(nw.at[here], nw_v.at[here], nw_o.at[here]) for here in (pl.ds(0, 256), pl.ds(256, 256))]
    ways += [(nm, nm_v, nm_o), (keys, keys_v, keys_o)]
    into = [pltpu.make_async_copy(a, v, i_sem.at[n]) for n, (a, v, _) in enumerate(ways)]
    out = [pltpu.make_async_copy(v, b, o_sem.at[n]) for n, (_, v, b) in enumerate(ways)]
    for cp in into:
        cp.start()
    for cp, back in zip(into, out):
        cp.wait()
        back.start()
    for back in out:
        back.wait()


def body(tokens, norm_gain, weight, momentum, cotangent, fragment, partner):
    hbm = pl.BlockSpec(memory_space=pltpu.HBM)
    V = pltpu.VMEM
    dma = pltpu.SemaphoreType.DMA
    shapes = (
        jax.ShapeDtypeStruct((128, 768), BF16),
        jax.ShapeDtypeStruct((512, 768), BF16),
        jax.ShapeDtypeStruct((512, HD), F32),
    )
    na, nb = NA * HD, (5 - NA) * HD
    outs = pl.pallas_call(
        kernel,
        out_shape=shapes,
        in_specs=[hbm] * 7,
        out_specs=(hbm,) * 3,
        scratch_shapes=[
            V((128, 8192), BF16),
            V((128, 128), F32),
            V((NC, 8, 128, 256), BF16),
            V((NC, 8, 128, 256), BF16),
            V((NC, 2, 128, 768), BF16),
            V((128, 768), BF16),
            V((8, 128, HD), BF16), V((8, 128, na), BF16), V((8, 128, nb), BF16),
            V((NC, 2, 128, HD), F32), V((NC, 2, 128, na), F32), V((NC, 2, 128, nb), F32),
            V((NC, 128, HD), BF16), V((NC, 128, na), BF16), V((NC, 128, nb), BF16),
            V((NC, 128, HD), BF16), V((NC, 128, na), BF16), V((NC, 128, nb), BF16),
            V((8, 128, 768), F32),
            V((4, 128, 768), BF16),
            V((4, 128, 768), BF16),
            V((4, 128, 768), BF16),
            V((3, 128, 768), BF16),
            V((NC, 8, 16, HD), BF16),
            V((32, 16, HD), BF16),
            V((32, 16, HD), BF16),
            V((NC, 8, 16, HD), BF16),
            V((512, HD), F32),
            V((8, HD), F32),
            V((1, 8192), F32),
            V((1, 32), jnp.int32),
            V((1, 32), jnp.int32),
            pltpu.SMEM((1, 32), jnp.int32),
            V((128, 768), BF16), V((512, 768), BF16), V((512, HD), F32),
            dma((12,)),
            dma((NC, 8)), dma((NC, 8)),
            dma((NC,)), dma((NC,)),
            dma((3, 4)), dma((3, 4)),
            dma((3, 4)), dma((3, 4)),
            dma((3, NC)), dma((3, NC)),
            dma, dma,
            dma((4,)), dma((4,)),
            dma, dma,
            dma, dma((NC,)),
            pltpu.SemaphoreType.REGULAR((4,)),
            dma((2, NC)),
        ],
        compiler_params=pltpu.CompilerParams(
            collective_id=0, has_side_effects=True, vmem_limit_bytes=62 * 2**20
        ),
    )(tokens[0], norm_gain[None], weight[0].reshape(NC, 128, 768), momentum[0], cotangent[0], fragment[None], partner[None])
    keys, nw, nm = pl.pallas_call(
        finish,
        out_shape=shapes,
        in_specs=[hbm] * 3,
        out_specs=(hbm,) * 3,
        scratch_shapes=[V((128, 768), BF16), V((512, 768), BF16), V((512, HD), F32), dma((4,)), dma((4,))],
        compiler_params=pltpu.CompilerParams(vmem_limit_bytes=62 * 2**20),
    )(*outs)
    return (keys[None], nw[None], nm[None])


def solution(mesh):
    in_specs = (
        P("replica", "fsdp", None),
        P(),
        P("replica", "fsdp", None),
        P("replica", "fsdp", None),
        P("replica", "fsdp", None),
        P(),
        P(),
    )
    out_specs = (P("replica", "fsdp", None), P("replica", "fsdp", None), P("replica", "fsdp", None))
    return jax.shard_map(body, mesh=mesh, in_specs=in_specs, out_specs=out_specs, check_vma=False)
```

```python
import jax
import jax.numpy as jnp
from jax import lax
from jax.experimental import pallas as pl
from jax.experimental.pallas import tpu as pltpu
from jax.sharding import PartitionSpec as P

HD = 128
NC = 4
NA = 1
MESH = pl.DeviceIdType.MESH
F32 = jnp.float32
BF16 = jnp.bfloat16

inner_rate = 0.0001
outer_rate = 0.7
beta_value = 0.9


def kernel(
    tokens, gain_h, weight, momentum, cot, fragment_h, partner_h,
    keys_o, nw_o, nm_o,
    tok, scale, S, R, W2, Cl, Cf, Ca, Cb, Gtf, Gta, Gtb, Gsf, Gsa, Gsb, Grf, Gra, Grb, Pacc, Ps, Pr, Ss, Sr,
    D, X1, X2s, X2r, mom, fragv, gain, fragment, partner_row, partner, keys_v, nw_v, nm_v,
    lsem, a_s, a_r, w_s, w_r, c_s, c_r, f_s, f_r, g_s, g_r, p_s, p_r, k_s, k_r, x1_s, x1_r, x2_s, x2_r, near, o_sem,
):
    r = lax.axis_index("replica")
    f = lax.axis_index("fsdp")
    xh = f // 8
    q = f % 8
    y = q // 2
    c = q % 2
    z = r // 2
    C = (Cf, Ca, Cb)
    Gt = (Gtf, Gta, Gtb)
    Gs = (Gsf, Gsa, Gsb)
    Gr = (Grf, Gra, Grb)

    def dev(q2):
        return (r, xh * 8 + q2)

    xpart = (r, (1 - xh) * 8 + q)
    sib = dev(y * 2 + 1 - c)

    small = [
        pltpu.make_async_copy(a, b, lsem.at[n])
        for n, (a, b) in enumerate(((fragment_h, fragment), (partner_h, partner_row), (partner_h, partner), (gain_h, gain)))
    ]
    c_cp = pltpu.make_async_copy(cot, Cl, lsem.at[4])
    w_cp = pltpu.make_async_copy(weight, W2.at[:, xh], lsem.at[5])
    m_cp = pltpu.make_async_copy(momentum, mom, lsem.at[6])
    tok_cp = [
        pltpu.make_async_copy(tokens.at[pl.ds(h * 32, 32)], tok.at[pl.ds(h * 32, 32)], lsem.at[7 + h])
        for h in range(4)
    ]
    for cp in [*small, c_cp, *tok_cp, w_cp, m_cp]:
        cp.start()

    bar = pltpu.get_barrier_semaphore()
    for k in range(1, 8):
        pl.semaphore_signal(bar, inc=1, device_id=dev((q + k) % 8), device_id_type=MESH)
    pl.semaphore_signal(bar, inc=1, device_id=xpart, device_id_type=MESH)

    pl.semaphore_signal(bar, inc=1, device_id=(z * 2 + 1 - r % 2, f), device_id_type=MESH)

    def in_line(away):
        return (z + away >= 0) & (z + away < 16)

    for away in (-1, 1):
        @pl.when(in_line(away))
        def _():
            for h in range(2):
                pl.semaphore_signal(bar, inc=1, device_id=((z + away) * 2 + h, f), device_id_type=MESH)

    def tell(level):
        far = 2 ** level
        for away in (-far, far):
            @pl.when(in_line(away))
            def _():
                pl.semaphore_signal(near.at[level], inc=1, device_id=(r + 2 * away, f), device_id_type=MESH)

    def hear(level):
        far = 2 ** level
        pl.semaphore_wait(near.at[level], jnp.minimum(z // far, 1) + jnp.minimum((15 - z) // far, 1))

    for cp in small:
        cp.wait()
    lane = lax.broadcasted_iota(jnp.int32, (8, 32), 1).astype(F32)
    mine = r.astype(F32)
    partners = jnp.broadcast_to(partner_row[...].astype(F32), (8, 32))
    mate = jnp.sum(jnp.where(lane == mine, partners, 0.0), axis=-1, keepdims=True)
    fragments = jnp.broadcast_to(fragment[...].astype(F32), (8, 32))
    frag_at = jnp.sum(jnp.where(lane == jnp.minimum(mate, mine), fragments, 0.0), axis=-1, keepdims=True)
    fragv[...] = jnp.broadcast_to(frag_at, (8, HD))

    c_cp.wait()
    frag = jnp.broadcast_to(fragv[0:1, :], (128, HD))
    blocks = [Cl[:, j * HD:(j + 1) * HD].astype(F32) for j in range(6)]
    cut = blocks[0]
    for j in range(1, 6):
        cut = jnp.where(frag == float(j), blocks[j], cut)
    Cf[q] = cut.astype(BF16)
    for m in range(5):
        rest = jnp.where(frag <= float(m), blocks[m + 1], blocks[m]).astype(BF16)
        if m < NA:
            Ca[q, :, m * HD:(m + 1) * HD] = rest
        else:
            Cb[q, :, (m - NA) * HD:(m - NA + 1) * HD] = rest

    def rows(t, _):
        here = pl.ds(pl.multiple_of(t * 16, 16), 16)
        v = tok[here, :].astype(F32)
        m = jnp.sum(v * v, axis=-1, keepdims=True) * (1.0 / 8192)
        scale[here, :] = jnp.broadcast_to(lax.rsqrt(m + 1e-05), (16, 128))
        return 0

    for h, cp in enumerate(tok_cp):
        cp.wait()
        lax.fori_loop(2 * h, 2 * h + 2, rows, 0)

    def a_send(i, k):
        q2 = (q + k) % 8
        return pltpu.make_async_remote_copy(
            src_ref=S.at[i, q2], dst_ref=R.at[i, q], send_sem=a_s.at[i, k], recv_sem=a_r.at[i, k], device_id=dev(q2),
            device_id_type=MESH)

    def norm_chunk(i):
        def one(b, _):
            for h in range(2):
                col = pl.multiple_of(h * 4096 + b * 512 + i * 128, 128)
                v = tok[:, pl.ds(col, 128)].astype(F32)
                S[i, b, :, h * 128:(h + 1) * 128] = (v * scale[...] * gain[:, pl.ds(col, 128)]).astype(BF16)
            return 0

        lax.fori_loop(0, 8, one, 0)
        R[i, q] = S[i, q]

    def send_chunk(i):
        def one(k, _):
            a_send(i, k).start()
            return 0

        lax.fori_loop(1, 8, one, 0)

    def c_send(g, k):
        to = sib if k == 0 else dev(((y + k) % 4) * 2 + c)
        return pltpu.make_async_remote_copy(
            src_ref=C[g].at[q], dst_ref=C[g].at[q], send_sem=c_s.at[g, k], recv_sem=c_r.at[g, k], device_id=to,
            device_id_type=MESH)

    def c_pass(g, k):
        slot = ((y + 4 - k) % 4) * 2 + c
        return pltpu.make_async_remote_copy(
            src_ref=C[g].at[slot], dst_ref=C[g].at[slot], send_sem=f_s.at[g, k], recv_sem=f_r.at[g, k], device_id=sib,
            device_id_type=MESH)

    def spread(g):
        for k in (2, 1, 3, 0):
            c_send(g, k).start()

    def collect(g):
        for k in (1, 3, 2):
            c_send(g, k).wait_recv()
            c_pass(g, k).start()
        c_send(g, 0).wait_recv()
        for k in (1, 3, 2):
            c_pass(g, k).wait_recv()

    def w_send(i):
        return pltpu.make_async_remote_copy(
            src_ref=W2.at[i, xh], dst_ref=W2.at[i, xh], send_sem=w_s.at[i], recv_sem=w_r.at[i], device_id=xpart,
            device_id_type=MESH)

    norm_chunk(0)
    w_cp.wait()
    pl.semaphore_wait(bar, 9 + 2 * jnp.minimum(z, 1) + 2 * jnp.minimum(15 - z, 1))

    spread(0)
    send_chunk(0)
    for i in range(NC):
        w_send(i).start()
    norm_chunk(1)
    send_chunk(1)
    tell(0)
    norm_chunk(2)
    norm_chunk(3)
    collect(0)
    hear(0)
    tell(1)

    def g_send(g, i):
        return pltpu.make_async_remote_copy(
            src_ref=Gs[g].at[i], dst_ref=Gr[g].at[i], send_sem=g_s.at[g, i], recv_sem=g_r.at[g, i], device_id=xpart,
            device_id_type=MESH)

    def grads(g, i):
        lhs = R[i].reshape(1024, 256)
        width = C[g].shape[-1]
        for n in range(0, width, 256):
            cols = slice(n, min(n + 256, width))
            wide = cols.stop - cols.start
            d = lax.dot_general(
                lhs, C[g][:, :, cols].reshape(1024, wide), (((0,), (0,)), ((), ())), preferred_element_type=F32)
            Gt[g][i, :, :, cols] = d.reshape(2, 128, wide)
        Gs[g][i] = Gt[g][i, 1 - xh].astype(BF16)
        g_send(g, i).start()

    def x1_send(i, k):
        j = ((i // 2) * 8 + 2 * (k // 2) + i % 2) * 2 + k % 2
        return j, pltpu.make_async_remote_copy(
            src_ref=D.at[i, k], dst_ref=X1.at[r], send_sem=x1_s, recv_sem=x1_r, device_id=(j, f), device_id_type=MESH)

    def offer(i):
        g_send(0, i).wait_recv()
        d = inner_rate * (Gtf[i, xh] + Grf[i].astype(F32))
        D[i] = d.astype(BF16).reshape(8, 16, HD)

        def one(k, _):
            j, cp = x1_send(i, k)

            @pl.when(j != r)
            def _():
                cp.start()

            @pl.when(j == r)
            def _():
                X1[r] = D[i, k]

            return 0

        lax.fori_loop(0, 8, one, 0)

    def offers(first, last):
        def one(i, _):
            offer(i)
            return 0

        lax.fori_loop(first, last, one, 0)

    my_chunk = 2 * (z // 8) + z % 2
    my_piece = 2 * ((z % 8) // 2) + r % 2

    def x2_send(d):
        return pltpu.make_async_remote_copy(
            src_ref=X2s.at[d], dst_ref=X2r.at[my_chunk, my_piece], send_sem=x2_s, recv_sem=x2_r.at[my_chunk],
            device_id=(d, f), device_id_type=MESH)

    def relay():
        whole = X1.at[pl.ds(0, 31)]
        pltpu.make_async_copy(whole, whole, x1_r).wait()

        def one(d, _):
            X2s[d] = X1[partner[0, d]]

            @pl.when(d != r)
            def _():
                x2_send(d).start()

            return 0

        lax.fori_loop(0, 32, one, 0)
        X2r[my_chunk, my_piece] = X2s[r]

    def step(t, _):
        def arrive(k, _):
            a_send(t, k).wait_recv()
            return 0

        lax.fori_loop(1, 8, arrive, 0)

        @pl.when(t == 0)
        def _():
            spread(1)
            send_chunk(2)

        @pl.when(t == 1)
        def _():
            send_chunk(3)

        grads(0, t)

        w_send(t).wait_recv()

        @pl.when(t == 0)
        def _():
            Pacc[...] = jnp.zeros_like(Pacc)

        lhs = R[t].reshape(1024, 256)
        for n in range(3):
            cols = slice(n * 256, (n + 1) * 256)
            p = jnp.dot(lhs, W2[t, :, :, cols].reshape(256, 256), preferred_element_type=F32)
            Pacc[:, :, cols] += p.reshape(8, 128, 256)

        @pl.when(t == 0)
        def _():
            hear(1)
            tell(2)

        @pl.when(t == 1)
        def _():
            hear(2)
            tell(3)

        @pl.when(t == 2)
        def _():
            spread(2)
            collect(1)

            def early(i, _):
                grads(1, i)
                return 0

            lax.fori_loop(0, NC - 1, early, 0)
            hear(3)
            offers(0, NC - 2)

        return 0

    lax.fori_loop(0, NC, step, 0)

    p_send = pltpu.make_async_remote_copy(
        src_ref=Ps, dst_ref=Pr, send_sem=p_s, recv_sem=p_r, device_id=sib, device_id_type=MESH)
    for b in range(4):
        Ps[b] = Pacc[b * 2 + 1 - c].astype(BF16)
    p_send.start()
    offers(NC - 2, NC)
    grads(1, NC - 1)

    def k_send(k):
        y2 = (y + k) % 4
        return pltpu.make_async_remote_copy(
            src_ref=Ss.at[y2], dst_ref=Sr.at[k - 1], send_sem=k_s.at[k], recv_sem=k_r.at[k], device_id=dev(y2 * 2 + c),
            device_id_type=MESH)

    p_send.wait_recv()
    for k in (2, 1, 3):
        y2 = (y + k) % 4
        Ss[y2] = (Pacc[y2 * 2 + c] + Pr[y2].astype(F32)).astype(BF16)
        k_send(k).start()

    collect(2)

    def late(i, _):
        grads(2, i)
        return 0

    lax.fori_loop(0, NC, late, 0)

    relay()

    for k in (1, 3, 2):
        k_send(k).wait_recv()
    own = Pacc[q] + Pr[y].astype(F32)
    keys_v[...] = (own + Sr[0].astype(F32) + Sr[1].astype(F32) + Sr[2].astype(F32)).astype(BF16)
    keys_cp = pltpu.make_async_copy(keys_v, keys_o, lsem.at[11])
    keys_cp.start()

    m_cp.wait()

    def inner(i, _):
        g_send(1, i).wait_recv()
        g_send(2, i).wait_recv()
        here = pl.ds(pl.multiple_of(i * 128, 128), 128)
        at = jnp.broadcast_to(fragv[0:1, :], (128, HD))

        def rest(m):
            g, n = (1, m) if m < NA else (2, m - NA)
            cols = slice(n * HD, (n + 1) * HD)
            return Gt[g][i, xh, :, cols] + Gr[g][i, :, cols].astype(F32)

        grads_of = [rest(m) for m in range(5)]
        for j in range(6):
            if j == 0:
                g = grads_of[0]
            elif j == 5:
                g = grads_of[4]
            else:
                g = jnp.where(at < float(j), grads_of[j - 1], grads_of[j])
            cols = slice(j * HD, (j + 1) * HD)
            nw_v[here, cols] = (W2[i, xh, :, cols].astype(F32) - inner_rate * g).astype(BF16)
        return 0

    lax.fori_loop(0, NC, inner, 0)

    def out_copies(i):
        here = pl.ds(pl.multiple_of(i * 128, 128), 128)
        return (
            pltpu.make_async_copy(nw_v.at[here], nw_o.at[here], o_sem.at[0, i]),
            pltpu.make_async_copy(nm_v.at[here], nm_o.at[here], o_sem.at[1, i]),
        )

    def update(i, _):
        @pl.when(my_chunk == i)
        def _():
            part = X2r.at[i, pl.ds(0, 7)]
            pltpu.make_async_copy(part, part, x2_r.at[i]).wait()

        @pl.when(my_chunk != i)
        def _():
            part = X2r.at[i]
            pltpu.make_async_copy(part, part, x2_r.at[i]).wait()

        here = pl.ds(pl.multiple_of(i * 128, 128), 128)
        delta = D[i].reshape(128, HD).astype(F32)
        mix = (delta + X2r[i].reshape(128, HD).astype(F32)) * 0.5
        nm = beta_value * mom[here, :] + mix
        nm_v[here, :] = nm
        step_out = outer_rate * (beta_value * nm + mix)
        at = jnp.broadcast_to(fragv[0:1, :], (128, HD))
        for j in range(6):
            cols = slice(j * HD, (j + 1) * HD)
            outer = W2[i, xh, :, cols].astype(F32) - step_out
            nw_v[here, cols] = jnp.where(at == float(j), outer, nw_v[here, cols].astype(F32)).astype(BF16)
        for cp in out_copies(i):
            cp.start()
        return 0

    lax.fori_loop(0, NC, update, 0)

    for k in range(4):
        for g in range(3):
            c_send(g, k).wait_send()
            if k > 0:
                c_pass(g, k).wait_send()
        if k > 0:
            k_send(k).wait_send()
    p_send.wait_send()

    def sent(i, _):
        w_send(i).wait_send()
        for g in range(3):
            g_send(g, i).wait_send()

        def one(k, _):
            a_send(i, k).wait_send()
            return 0

        lax.fori_loop(1, 8, one, 0)
        return 0

    lax.fori_loop(0, NC, sent, 0)
    most = X1.at[pl.ds(0, 31)]
    pltpu.make_async_copy(most, most, x1_s).wait()
    pltpu.make_async_copy(most, most, x2_s).wait()
    keys_cp.wait()

    def written(i, _):
        for cp in out_copies(i):
            cp.wait()
        return 0

    lax.fori_loop(0, NC, written, 0)


def finish(keys, nw, nm, keys_o, nw_o, nm_o, keys_v, nw_v, nm_v, i_sem, o_sem):
    ways = [(nw.at[here], nw_v.at[here], nw_o.at[here]) for here in (pl.ds(0, 256), pl.ds(256, 256))]
    ways += [(nm, nm_v, nm_o), (keys, keys_v, keys_o)]
    into = [pltpu.make_async_copy(a, v, i_sem.at[n]) for n, (a, v, _) in enumerate(ways)]
    out = [pltpu.make_async_copy(v, b, o_sem.at[n]) for n, (_, v, b) in enumerate(ways)]
    for cp in into:
        cp.start()
    for cp, back in zip(into, out):
        cp.wait()
        back.start()
    for back in out:
        back.wait()


def body(tokens, norm_gain, weight, momentum, cotangent, fragment, partner):
    hbm = pl.BlockSpec(memory_space=pltpu.HBM)
    V = pltpu.VMEM
    dma = pltpu.SemaphoreType.DMA
    shapes = (
        jax.ShapeDtypeStruct((128, 768), BF16),
        jax.ShapeDtypeStruct((512, 768), BF16),
        jax.ShapeDtypeStruct((512, HD), F32),
    )
    na, nb = NA * HD, (5 - NA) * HD
    outs = pl.pallas_call(
        kernel,
        out_shape=shapes,
        in_specs=[hbm] * 7,
        out_specs=(hbm,) * 3,
        scratch_shapes=[
            V((128, 8192), BF16),
            V((128, 128), F32),
            V((NC, 8, 128, 256), BF16),
            V((NC, 8, 128, 256), BF16),
            V((NC, 2, 128, 768), BF16),
            V((128, 768), BF16),
            V((8, 128, HD), BF16), V((8, 128, na), BF16), V((8, 128, nb), BF16),
            V((NC, 2, 128, HD), F32), V((NC, 2, 128, na), F32), V((NC, 2, 128, nb), F32),
            V((NC, 128, HD), BF16), V((NC, 128, na), BF16), V((NC, 128, nb), BF16),
            V((NC, 128, HD), BF16), V((NC, 128, na), BF16), V((NC, 128, nb), BF16),
            V((8, 128, 768), F32),
            V((4, 128, 768), BF16),
            V((4, 128, 768), BF16),
            V((4, 128, 768), BF16),
            V((3, 128, 768), BF16),
            V((NC, 8, 16, HD), BF16),
            V((32, 16, HD), BF16),
            V((32, 16, HD), BF16),
            V((NC, 8, 16, HD), BF16),
            V((512, HD), F32),
            V((8, HD), F32),
            V((1, 8192), F32),
            V((1, 32), jnp.int32),
            V((1, 32), jnp.int32),
            pltpu.SMEM((1, 32), jnp.int32),
            V((128, 768), BF16), V((512, 768), BF16), V((512, HD), F32),
            dma((12,)),
            dma((NC, 8)), dma((NC, 8)),
            dma((NC,)), dma((NC,)),
            dma((3, 4)), dma((3, 4)),
            dma((3, 4)), dma((3, 4)),
            dma((3, NC)), dma((3, NC)),
            dma, dma,
            dma((4,)), dma((4,)),
            dma, dma,
            dma, dma((NC,)),
            pltpu.SemaphoreType.REGULAR((4,)),
            dma((2, NC)),
        ],
        compiler_params=pltpu.CompilerParams(
            collective_id=0, has_side_effects=True, vmem_limit_bytes=62 * 2**20
        ),
    )(tokens[0], norm_gain[None], weight[0].reshape(NC, 128, 768), momentum[0], cotangent[0], fragment[None], partner[None])
    keys, nw, nm = pl.pallas_call(
        finish,
        out_shape=shapes,
        in_specs=[hbm] * 3,
        out_specs=(hbm,) * 3,
        scratch_shapes=[V((128, 768), BF16), V((512, 768), BF16), V((512, HD), F32), dma((4,)), dma((4,))],
        compiler_params=pltpu.CompilerParams(vmem_limit_bytes=62 * 2**20),
    )(*outs)
    return (keys[None], nw[None], nm[None])


def solution(mesh):
    in_specs = (
        P("replica", "fsdp", None),
        P(),
        P("replica", "fsdp", None),
        P("replica", "fsdp", None),
        P("replica", "fsdp", None),
        P(),
        P(),
    )
    out_specs = (P("replica", "fsdp", None), P("replica", "fsdp", None), P("replica", "fsdp", None))
    return jax.shard_map(body, mesh=mesh, in_specs=in_specs, out_specs=out_specs, check_vma=False)
```

```python
import jax
import jax.numpy as jnp
from jax import lax
from jax.experimental import pallas as pl
from jax.experimental.pallas import tpu as pltpu
from jax.sharding import PartitionSpec as P

HD = 128
NC = 4
NA = 1
MESH = pl.DeviceIdType.MESH
F32 = jnp.float32
BF16 = jnp.bfloat16

inner_rate = 0.0001
outer_rate = 0.7
beta_value = 0.9


def kernel(
    tokens, gain_h, weight, momentum, cot, fragment_h, partner_h,
    keys_o, nw_o, nm_o,
    tok, scale, S, R, W2, Cl, Cf, Ca, Cb, Gtf, Gta, Gtb, Gsf, Gsa, Gsb, Grf, Gra, Grb, Pacc, Ps, Pr, Ss, Sr,
    D, X1, X2s, X2r, mom, fragv, gain, fragment, partner_row, partner, keys_v, nw_v, nm_v,
    lsem, a_s, a_r, w_s, w_r, c_s, c_r, f_s, f_r, g_s, g_r, p_s, p_r, k_s, k_r, x1_s, x1_r, x2_s, x2_r, near, o_sem,
):
    r = lax.axis_index("replica")
    f = lax.axis_index("fsdp")
    xh = f // 8
    q = f % 8
    y = q // 2
    c = q % 2
    z = r // 2
    C = (Cf, Ca, Cb)
    Gt = (Gtf, Gta, Gtb)
    Gs = (Gsf, Gsa, Gsb)
    Gr = (Grf, Gra, Grb)

    def dev(q2):
        return (r, xh * 8 + q2)

    xpart = (r, (1 - xh) * 8 + q)
    sib = dev(y * 2 + 1 - c)

    small = [
        pltpu.make_async_copy(a, b, lsem.at[n])
        for n, (a, b) in enumerate(((fragment_h, fragment), (partner_h, partner_row), (partner_h, partner), (gain_h, gain)))
    ]
    c_cp = pltpu.make_async_copy(cot, Cl, lsem.at[4])
    w_cp = pltpu.make_async_copy(weight, W2.at[:, xh], lsem.at[5])
    m_cp = pltpu.make_async_copy(momentum, mom, lsem.at[6])
    tok_cp = [
        pltpu.make_async_copy(tokens.at[pl.ds(h * 32, 32)], tok.at[pl.ds(h * 32, 32)], lsem.at[7 + h])
        for h in range(4)
    ]
    for cp in [*small, c_cp, *tok_cp, w_cp, m_cp]:
        cp.start()

    bar = pltpu.get_barrier_semaphore()
    for k in range(1, 8):
        pl.semaphore_signal(bar, inc=1, device_id=dev((q + k) % 8), device_id_type=MESH)
    pl.semaphore_signal(bar, inc=1, device_id=xpart, device_id_type=MESH)

    pl.semaphore_signal(bar, inc=1, device_id=(z * 2 + 1 - r % 2, f), device_id_type=MESH)

    def in_line(away):
        return (z + away >= 0) & (z + away < 16)

    for away in (-1, 1):
        @pl.when(in_line(away))
        def _():
            for h in range(2):
                pl.semaphore_signal(bar, inc=1, device_id=((z + away) * 2 + h, f), device_id_type=MESH)

    def tell(level):
        far = 2 ** level
        for away in (-far, far):
            @pl.when(in_line(away))
            def _():
                pl.semaphore_signal(near.at[level], inc=1, device_id=(r + 2 * away, f), device_id_type=MESH)

    def hear(level):
        far = 2 ** level
        pl.semaphore_wait(near.at[level], jnp.minimum(z // far, 1) + jnp.minimum((15 - z) // far, 1))

    for cp in small:
        cp.wait()
    lane = lax.broadcasted_iota(jnp.int32, (8, 32), 1).astype(F32)
    mine = r.astype(F32)
    partners = jnp.broadcast_to(partner_row[...].astype(F32), (8, 32))
    mate = jnp.sum(jnp.where(lane == mine, partners, 0.0), axis=-1, keepdims=True)
    fragments = jnp.broadcast_to(fragment[...].astype(F32), (8, 32))
    frag_at = jnp.sum(jnp.where(lane == jnp.minimum(mate, mine), fragments, 0.0), axis=-1, keepdims=True)
    fragv[...] = jnp.broadcast_to(frag_at, (8, HD))

    c_cp.wait()
    frag = jnp.broadcast_to(fragv[0:1, :], (128, HD))
    blocks = [Cl[:, j * HD:(j + 1) * HD].astype(F32) for j in range(6)]
    cut = blocks[0]
    for j in range(1, 6):
        cut = jnp.where(frag == float(j), blocks[j], cut)
    Cf[q] = cut.astype(BF16)
    for m in range(5):
        rest = jnp.where(frag <= float(m), blocks[m + 1], blocks[m]).astype(BF16)
        if m < NA:
            Ca[q, :, m * HD:(m + 1) * HD] = rest
        else:
            Cb[q, :, (m - NA) * HD:(m - NA + 1) * HD] = rest

    def rows(t, _):
        here = pl.ds(pl.multiple_of(t * 16, 16), 16)
        v = tok[here, :].astype(F32)
        m = jnp.sum(v * v, axis=-1, keepdims=True) * (1.0 / 8192)
        scale[here, :] = jnp.broadcast_to(lax.rsqrt(m + 1e-05), (16, 128))
        return 0

    for h, cp in enumerate(tok_cp):
        cp.wait()
        lax.fori_loop(2 * h, 2 * h + 2, rows, 0)

    def a_send(i, k):
        q2 = (q + k) % 8
        return pltpu.make_async_remote_copy(
            src_ref=S.at[i, q2], dst_ref=R.at[i, q], send_sem=a_s.at[i, k], recv_sem=a_r.at[i, k], device_id=dev(q2),
            device_id_type=MESH)

    def norm_chunk(i):
        def one(b, _):
            for h in range(2):
                col = pl.multiple_of(h * 4096 + b * 512 + i * 128, 128)
                v = tok[:, pl.ds(col, 128)].astype(F32)
                S[i, b, :, h * 128:(h + 1) * 128] = (v * scale[...] * gain[:, pl.ds(col, 128)]).astype(BF16)
            return 0

        lax.fori_loop(0, 8, one, 0)
        R[i, q] = S[i, q]

    def send_chunk(i):
        def one(k, _):
            a_send(i, k).start()
            return 0

        lax.fori_loop(1, 8, one, 0)

    def c_send(g, k):
        to = sib if k == 0 else dev(((y + k) % 4) * 2 + c)
        return pltpu.make_async_remote_copy(
            src_ref=C[g].at[q], dst_ref=C[g].at[q], send_sem=c_s.at[g, k], recv_sem=c_r.at[g, k], device_id=to,
            device_id_type=MESH)

    def c_pass(g, k):
        slot = ((y + 4 - k) % 4) * 2 + c
        return pltpu.make_async_remote_copy(
            src_ref=C[g].at[slot], dst_ref=C[g].at[slot], send_sem=f_s.at[g, k], recv_sem=f_r.at[g, k], device_id=sib,
            device_id_type=MESH)

    def spread(g):
        for k in (2, 1, 3, 0):
            c_send(g, k).start()

    def collect(g):
        for k in (1, 3, 2):
            c_send(g, k).wait_recv()
            c_pass(g, k).start()
        c_send(g, 0).wait_recv()
        for k in (1, 3, 2):
            c_pass(g, k).wait_recv()

    def w_send(i):
        return pltpu.make_async_remote_copy(
            src_ref=W2.at[i, xh], dst_ref=W2.at[i, xh], send_sem=w_s.at[i], recv_sem=w_r.at[i], device_id=xpart,
            device_id_type=MESH)

    norm_chunk(0)
    w_cp.wait()
    pl.semaphore_wait(bar, 9 + 2 * jnp.minimum(z, 1) + 2 * jnp.minimum(15 - z, 1))

    spread(0)
    send_chunk(0)
    for i in range(NC):
        w_send(i).start()
    norm_chunk(1)
    send_chunk(1)
    tell(0)
    norm_chunk(2)
    norm_chunk(3)
    collect(0)
    hear(0)
    tell(1)

    def g_send(g, i):
        return pltpu.make_async_remote_copy(
            src_ref=Gs[g].at[i], dst_ref=Gr[g].at[i], send_sem=g_s.at[g, i], recv_sem=g_r.at[g, i], device_id=xpart,
            device_id_type=MESH)

    def grads(g, i):
        lhs = R[i].reshape(1024, 256)
        width = C[g].shape[-1]
        for n in range(0, width, 256):
            cols = slice(n, min(n + 256, width))
            wide = cols.stop - cols.start
            d = lax.dot_general(
                lhs, C[g][:, :, cols].reshape(1024, wide), (((0,), (0,)), ((), ())), preferred_element_type=F32)
            Gt[g][i, :, :, cols] = d.reshape(2, 128, wide)
        Gs[g][i] = Gt[g][i, 1 - xh].astype(BF16)
        g_send(g, i).start()

    def x1_send(i, k):
        j = ((i // 2) * 8 + 2 * (k // 2) + i % 2) * 2 + k % 2
        return j, pltpu.make_async_remote_copy(
            src_ref=D.at[i, k], dst_ref=X1.at[r], send_sem=x1_s, recv_sem=x1_r, device_id=(j, f), device_id_type=MESH)

    def offer(i):
        g_send(0, i).wait_recv()
        d = inner_rate * (Gtf[i, xh] + Grf[i].astype(F32))
        D[i] = d.astype(BF16).reshape(8, 16, HD)

        def one(k, _):
            j, cp = x1_send(i, k)

            @pl.when(j != r)
            def _():
                cp.start()

            @pl.when(j == r)
            def _():
                X1[r] = D[i, k]

            return 0

        lax.fori_loop(0, 8, one, 0)

    def offers(first, last):
        def one(i, _):
            offer(i)
            return 0

        lax.fori_loop(first, last, one, 0)

    my_chunk = 2 * (z // 8) + z % 2
    my_piece = 2 * ((z % 8) // 2) + r % 2

    def x2_send(d):
        return pltpu.make_async_remote_copy(
            src_ref=X2s.at[d], dst_ref=X2r.at[my_chunk, my_piece], send_sem=x2_s, recv_sem=x2_r.at[my_chunk],
            device_id=(d, f), device_id_type=MESH)

    def relay():
        whole = X1.at[pl.ds(0, 31)]
        pltpu.make_async_copy(whole, whole, x1_r).wait()

        def one(d, _):
            X2s[d] = X1[partner[0, d]]

            @pl.when(d != r)
            def _():
                x2_send(d).start()

            return 0

        lax.fori_loop(0, 32, one, 0)
        X2r[my_chunk, my_piece] = X2s[r]

    def step(t, _):
        def arrive(k, _):
            a_send(t, k).wait_recv()
            return 0

        lax.fori_loop(1, 8, arrive, 0)

        @pl.when(t == 0)
        def _():
            spread(1)
            send_chunk(2)

        @pl.when(t == 1)
        def _():
            send_chunk(3)

        grads(0, t)

        w_send(t).wait_recv()

        @pl.when(t == 0)
        def _():
            Pacc[...] = jnp.zeros_like(Pacc)

        lhs = R[t].reshape(1024, 256)
        for n in range(3):
            cols = slice(n * 256, (n + 1) * 256)
            p = jnp.dot(lhs, W2[t, :, :, cols].reshape(256, 256), preferred_element_type=F32)
            Pacc[:, :, cols] += p.reshape(8, 128, 256)

        @pl.when(t == 0)
        def _():
            hear(1)
            tell(2)

        @pl.when(t == 1)
        def _():
            hear(2)
            tell(3)

        @pl.when(t == 2)
        def _():
            spread(2)
            collect(1)

            def early(i, _):
                grads(1, i)
                return 0

            lax.fori_loop(0, NC - 1, early, 0)
            hear(3)
            offers(0, NC - 2)

        return 0

    lax.fori_loop(0, NC, step, 0)

    p_send = pltpu.make_async_remote_copy(
        src_ref=Ps, dst_ref=Pr, send_sem=p_s, recv_sem=p_r, device_id=sib, device_id_type=MESH)
    for b in range(4):
        Ps[b] = Pacc[b * 2 + 1 - c].astype(BF16)
    p_send.start()
    offers(NC - 2, NC)
    grads(1, NC - 1)

    def k_send(k):
        y2 = (y + k) % 4
        return pltpu.make_async_remote_copy(
            src_ref=Ss.at[y2], dst_ref=Sr.at[k - 1], send_sem=k_s.at[k], recv_sem=k_r.at[k], device_id=dev(y2 * 2 + c),
            device_id_type=MESH)

    p_send.wait_recv()
    for k in (2, 1, 3):
        y2 = (y + k) % 4
        Ss[y2] = (Pacc[y2 * 2 + c] + Pr[y2].astype(F32)).astype(BF16)
        k_send(k).start()

    collect(2)

    def late(i, _):
        grads(2, i)
        return 0

    lax.fori_loop(0, NC, late, 0)

    relay()

    for k in (1, 3, 2):
        k_send(k).wait_recv()
    own = Pacc[q] + Pr[y].astype(F32)
    keys_v[...] = (own + Sr[0].astype(F32) + Sr[1].astype(F32) + Sr[2].astype(F32)).astype(BF16)
    keys_cp = pltpu.make_async_copy(keys_v, keys_o, lsem.at[11])
    keys_cp.start()

    m_cp.wait()

    def inner(i, _):
        g_send(1, i).wait_recv()
        g_send(2, i).wait_recv()
        here = pl.ds(pl.multiple_of(i * 128, 128), 128)
        at = jnp.broadcast_to(fragv[0:1, :], (128, HD))

        def rest(m):
            g, n = (1, m) if m < NA else (2, m - NA)
            cols = slice(n * HD, (n + 1) * HD)
            return Gt[g][i, xh, :, cols] + Gr[g][i, :, cols].astype(F32)

        grads_of = [rest(m) for m in range(5)]
        for j in range(6):
            if j == 0:
                g = grads_of[0]
            elif j == 5:
                g = grads_of[4]
            else:
                g = jnp.where(at < float(j), grads_of[j - 1], grads_of[j])
            cols = slice(j * HD, (j + 1) * HD)
            nw_v[here, cols] = (W2[i, xh, :, cols].astype(F32) - inner_rate * g).astype(BF16)
        return 0

    lax.fori_loop(0, NC, inner, 0)

    for k in range(4):
        for g in range(3):
            c_send(g, k).wait_send()
            if k > 0:
                c_pass(g, k).wait_send()
        if k > 0:
            k_send(k).wait_send()
    p_send.wait_send()

    def sent(i, _):
        w_send(i).wait_send()
        for g in range(3):
            g_send(g, i).wait_send()

        def one(k, _):
            a_send(i, k).wait_send()
            return 0

        lax.fori_loop(1, 8, one, 0)
        return 0

    lax.fori_loop(0, NC, sent, 0)
    most = X1.at[pl.ds(0, 31)]
    pltpu.make_async_copy(most, most, x1_s).wait()

    def out_copies(i):
        here = pl.ds(pl.multiple_of(i * 128, 128), 128)
        return (
            pltpu.make_async_copy(nw_v.at[here], nw_o.at[here], o_sem.at[0, i]),
            pltpu.make_async_copy(nm_v.at[here], nm_o.at[here], o_sem.at[1, i]),
        )

    def update(i, _):
        @pl.when(my_chunk == i)
        def _():
            part = X2r.at[i, pl.ds(0, 7)]
            pltpu.make_async_copy(part, part, x2_r.at[i]).wait()

        @pl.when(my_chunk != i)
        def _():
            part = X2r.at[i]
            pltpu.make_async_copy(part, part, x2_r.at[i]).wait()

        here = pl.ds(pl.multiple_of(i * 128, 128), 128)
        delta = D[i].reshape(128, HD).astype(F32)
        mix = (delta + X2r[i].reshape(128, HD).astype(F32)) * 0.5
        nm = beta_value * mom[here, :] + mix
        nm_v[here, :] = nm
        step_out = outer_rate * (beta_value * nm + mix)
        at = jnp.broadcast_to(fragv[0:1, :], (128, HD))
        for j in range(6):
            cols = slice(j * HD, (j + 1) * HD)
            outer = W2[i, xh, :, cols].astype(F32) - step_out
            nw_v[here, cols] = jnp.where(at == float(j), outer, nw_v[here, cols].astype(F32)).astype(BF16)
        for cp in out_copies(i):
            cp.start()
        return 0

    lax.fori_loop(0, NC, update, 0)

    pltpu.make_async_copy(most, most, x2_s).wait()
    keys_cp.wait()

    def written(i, _):
        for cp in out_copies(i):
            cp.wait()
        return 0

    lax.fori_loop(0, NC, written, 0)


def finish(keys, nw, nm, keys_o, nw_o, nm_o, keys_v, nw_v, nm_v, i_sem, o_sem):
    ways = [(nw.at[here], nw_v.at[here], nw_o.at[here]) for here in (pl.ds(k * 128, 128) for k in range(4))]
    ways += [(nm, nm_v, nm_o), (keys, keys_v, keys_o)]
    into = [pltpu.make_async_copy(a, v, i_sem.at[n]) for n, (a, v, _) in enumerate(ways)]
    out = [pltpu.make_async_copy(v, b, o_sem.at[n]) for n, (_, v, b) in enumerate(ways)]
    for cp in into:
        cp.start()
    for cp, back in zip(into, out):
        cp.wait()
        back.start()
    for back in out:
        back.wait()


def body(tokens, norm_gain, weight, momentum, cotangent, fragment, partner):
    hbm = pl.BlockSpec(memory_space=pltpu.HBM)
    V = pltpu.VMEM
    dma = pltpu.SemaphoreType.DMA
    shapes = (
        jax.ShapeDtypeStruct((128, 768), BF16),
        jax.ShapeDtypeStruct((512, 768), BF16),
        jax.ShapeDtypeStruct((512, HD), F32),
    )
    na, nb = NA * HD, (5 - NA) * HD
    outs = pl.pallas_call(
        kernel,
        out_shape=shapes,
        in_specs=[hbm] * 7,
        out_specs=(hbm,) * 3,
        scratch_shapes=[
            V((128, 8192), BF16),
            V((128, 128), F32),
            V((NC, 8, 128, 256), BF16),
            V((NC, 8, 128, 256), BF16),
            V((NC, 2, 128, 768), BF16),
            V((128, 768), BF16),
            V((8, 128, HD), BF16), V((8, 128, na), BF16), V((8, 128, nb), BF16),
            V((NC, 2, 128, HD), F32), V((NC, 2, 128, na), F32), V((NC, 2, 128, nb), F32),
            V((NC, 128, HD), BF16), V((NC, 128, na), BF16), V((NC, 128, nb), BF16),
            V((NC, 128, HD), BF16), V((NC, 128, na), BF16), V((NC, 128, nb), BF16),
            V((8, 128, 768), F32),
            V((4, 128, 768), BF16),
            V((4, 128, 768), BF16),
            V((4, 128, 768), BF16),
            V((3, 128, 768), BF16),
            V((NC, 8, 16, HD), BF16),
            V((32, 16, HD), BF16),
            V((32, 16, HD), BF16),
            V((NC, 8, 16, HD), BF16),
            V((512, HD), F32),
            V((8, HD), F32),
            V((1, 8192), F32),
            V((1, 32), jnp.int32),
            V((1, 32), jnp.int32),
            pltpu.SMEM((1, 32), jnp.int32),
            V((128, 768), BF16), V((512, 768), BF16), V((512, HD), F32),
            dma((12,)),
            dma((NC, 8)), dma((NC, 8)),
            dma((NC,)), dma((NC,)),
            dma((3, 4)), dma((3, 4)),
            dma((3, 4)), dma((3, 4)),
            dma((3, NC)), dma((3, NC)),
            dma, dma,
            dma((4,)), dma((4,)),
            dma, dma,
            dma, dma((NC,)),
            pltpu.SemaphoreType.REGULAR((4,)),
            dma((2, NC)),
        ],
        compiler_params=pltpu.CompilerParams(
            collective_id=0, has_side_effects=True, vmem_limit_bytes=62 * 2**20
        ),
    )(tokens[0], norm_gain[None], weight[0].reshape(NC, 128, 768), momentum[0], cotangent[0], fragment[None], partner[None])
    keys, nw, nm = pl.pallas_call(
        finish,
        out_shape=shapes,
        in_specs=[hbm] * 3,
        out_specs=(hbm,) * 3,
        scratch_shapes=[V((128, 768), BF16), V((512, 768), BF16), V((512, HD), F32), dma((6,)), dma((6,))],
        compiler_params=pltpu.CompilerParams(vmem_limit_bytes=62 * 2**20),
    )(*outs)
    return (keys[None], nw[None], nm[None])


def solution(mesh):
    in_specs = (
        P("replica", "fsdp", None),
        P(),
        P("replica", "fsdp", None),
        P("replica", "fsdp", None),
        P("replica", "fsdp", None),
        P(),
        P(),
    )
    out_specs = (P("replica", "fsdp", None), P("replica", "fsdp", None), P("replica", "fsdp", None))
    return jax.shard_map(body, mesh=mesh, in_specs=in_specs, out_specs=out_specs, check_vma=False)
```
